128 devices in a mesh: group: 4 (over z), curve: 32 (over x, y, core).
Axes of the slice: x: 4, y: 4, z: 4, core: 2. Of those that a mesh axis runs over, the one named last changes fastest.
Arguments:
- moisture: float32 [72, 16, 131072], P(None, None, ('group', 'curve')), may hold values from -6 to 6
- jacobian: float32 [131072], P(('group', 'curve')), may hold values from 0.5 to 2
- partners: int32 [2, 131072], P(None, ('group', 'curve')), may hold values from 0 to 131071, as said below
- daylit: int32 [131072], P(('group', 'curve')), may hold values from 0 to 1, as said below
- cos_zenith: float32 [131072], P(('group', 'curve')), may hold values from 0.05 to 1
- albedo: float32 [131072], P(('group', 'curve')), may hold values from 0.05 to 0.8
- absorb: float32 [112, 72], replicated, may hold values from 0.002 to 0.2
- rayleigh: float32 [112], replicated, may hold values from 0.005 to 0.05
- solar: float32 [112], replicated, may hold values from 0.002 to 0.02
Outputs:
- moisture_new: float32 [72, 16, 131072], P(None, None, ('group', 'curve'))
- heating: float32 [72, 131072], P(None, ('group', 'curve'))
The draws below stay inside these ranges and needn't reach their ends.
Inputs may be any that keep to these rules, and one draw needn't show every extreme that they name: partners pairs elements of one group with each other (partner of partner is the element itself, never the element itself, the same for row 0 and row 1 separately); the partner of a group-local position p lies in the same block of 1024 consecutive positions that start at 512 + a multiple of 1024, taken cyclically in the group. Exactly 65536 elements are daylit in all; the groups' counts differ; within each group the daylit elements form one to three runs along the curve, and a run may wrap around the group's end.
All inputs are finite; a program needn't handle non-finite values.
Results may differ from the reference program's by a relative error of at most 0.000094.
Values sent between devices are 32-bit elements; how exact they have to be, the bound alone decides.
A program may use at most 192 MiB of HBM per device.

```python
import math
import jax
import jax.numpy as jnp
import numpy as np
from jax import lax

LEV = 72
G = 112
E_DEV = 1024
E_GROUP = 32768
ELEMS = 131072
N_GROUP = 4
N_CURVE = 32


def draw_partners(key, part):
    key = jax.random.fold_in(key, 11)
    e_group = E_DEV * N_CURVE
    shape_four = (2, N_GROUP, N_CURVE, E_DEV)
    scores = jax.random.randint(key, shape_four, 0, 1 << 16) * E_DEV + lax.broadcasted_iota(jnp.int32, shape_four, 3)
    shuffled = jnp.argsort(scores, axis=-1).astype(jnp.int32)
    flipped = jnp.arange(E_DEV, dtype=jnp.int32) ^ 1
    mate_slots = shuffled[..., flipped]
    inverse = jnp.argsort(shuffled, axis=-1).astype(jnp.int32)
    partner_slot = jnp.take_along_axis(mate_slots, inverse, axis=-1)
    half_width = E_DEV // 2
    window_base = lax.broadcasted_iota(jnp.int32, shape_four, 2) * E_DEV
    local_index = (window_base + half_width + partner_slot) % e_group
    flat_index = local_index.reshape(2, N_GROUP, e_group)
    placed = jnp.roll(flat_index, half_width, axis=-1)
    group_base = lax.broadcasted_iota(jnp.int32, (2, N_GROUP, e_group), 1) * e_group
    return (placed + group_base).reshape(2, N_GROUP * e_group).astype(jnp.int32)


def draw_daylit(key, part):
    key = jax.random.fold_in(key, 12)
    e_group = E_DEV * N_CURVE
    pair_count = N_GROUP // 2
    shift = jax.random.randint(jax.random.fold_in(key, 1), (pair_count, 1), e_group // 8, 3 * e_group // 8 + 1)
    flip = jax.random.randint(jax.random.fold_in(key, 2), (pair_count, 1), 0, 2) * 2 - 1
    signs = jnp.concatenate([flip, -flip], axis=1).reshape(N_GROUP, 1)
    deltas = jnp.concatenate([shift, shift], axis=1).reshape(N_GROUP, 1)
    lit_total = e_group // 2 + signs * deltas
    dark_total = e_group - lit_total
    run_count = jax.random.randint(jax.random.fold_in(key, 3), (N_GROUP, 1), 1, 4)
    second_on = (run_count >= 2).astype(jnp.int32)
    third_on = (run_count >= 3).astype(jnp.int32)
    lit_two = jax.random.randint(jax.random.fold_in(key, 4), (N_GROUP, 1), 1, lit_total // 4 + 1) * second_on
    lit_three = jax.random.randint(jax.random.fold_in(key, 5), (N_GROUP, 1), 1, lit_total // 4 + 1) * third_on
    lit_one = lit_total - lit_two - lit_three
    dark_two = jax.random.randint(jax.random.fold_in(key, 6), (N_GROUP, 1), 1, dark_total // 4 + 1) * second_on
    dark_three = jax.random.randint(jax.random.fold_in(key, 7), (N_GROUP, 1), 1, dark_total // 4 + 1) * third_on
    dark_one = dark_total - dark_two - dark_three
    first_lit = jax.random.randint(jax.random.fold_in(key, 8), (N_GROUP, 1), 0, e_group)
    position = lax.broadcasted_iota(jnp.int32, (N_GROUP, e_group), 1)
    offset = (position - first_lit) % e_group
    bound_one = lit_one
    bound_two = bound_one + dark_one
    bound_three = bound_two + lit_two
    bound_four = bound_three + dark_two
    bound_five = bound_four + lit_three
    in_one = offset < bound_one
    in_two = (offset >= bound_two) & (offset < bound_three)
    in_three = (offset >= bound_four) & (offset < bound_five)
    lit_flag = (in_one | in_two | in_three).astype(jnp.int32)
    return lit_flag.reshape(N_GROUP * e_group)


def block_levels(own_key, dims, shards, least, high):
    factor_of, own = 1.0, jax.random.fold_in(own_key, 6)
    for dim, parts in shards:
        steps = jnp.exp(jax.random.uniform(jax.random.fold_in(own, dim), (parts,), jnp.float32, least / len(shards), high / len(shards)))
        factor_of = factor_of * jnp.repeat(steps, dims[dim] // parts).reshape([-1 if axis == dim else 1 for axis in range(len(dims))])
    return factor_of


def noise(key, shape, width, most, pieces=(), kind=jnp.bfloat16):
    level = block_levels(key, shape, pieces, -0.22, 0.18) if pieces else 1.0
    result = jax.random.normal(key, shape, jnp.float32) * width * level
    return jnp.minimum(jnp.maximum(result, -most), most).astype(kind)


def setup_inputs(seed: int = 0) -> dict:
    seeds = jax.random.split(jax.random.key(seed), 10)
    return {
        "moisture": noise(seeds[0], (LEV, 16, ELEMS), 1.0, 6.0, ((2, 128),), jnp.float32),
        "jacobian": jnp.clip(jnp.exp(math.log(2.0) - 1.3862944 * jax.random.uniform(seeds[1], (ELEMS,), jnp.float32) ** block_levels(seeds[1], (ELEMS,), ((0, 128),), -0.2, 0.2)), 0.5, 2.0),
        "partners": draw_partners(jax.random.fold_in(seeds[9], 71), 0),
        "daylit": draw_daylit(jax.random.fold_in(seeds[9], 71), 0),
        "cos_zenith": jnp.clip(jnp.exp(math.log(1.0) - 2.9957323 * jax.random.uniform(seeds[4], (ELEMS,), jnp.float32) ** block_levels(seeds[4], (ELEMS,), ((0, 128),), -0.2, 0.2)), 0.05, 1.0),
        "albedo": jnp.clip(0.05 + 0.75 * jax.random.uniform(seeds[5], (ELEMS,), jnp.float32) ** block_levels(seeds[5], (ELEMS,), ((0, 128),), -0.2, 0.2), 0.05, 0.8),
        "absorb": jnp.clip(jnp.exp(jax.random.uniform(seeds[6], (G, LEV), jnp.float32, math.log(0.002), math.log(0.2))), 0.002, 0.2),
        "rayleigh": jnp.clip(jnp.exp(jax.random.uniform(seeds[7], (G,), jnp.float32, math.log(0.005), math.log(0.05))), 0.005, 0.05),
        "solar": jnp.clip(jnp.exp(jax.random.uniform(seeds[8], (G,), jnp.float32, math.log(0.002), math.log(0.02))), 0.002, 0.02),
    }


edge_nodes = np.array([4, 8, 7, 11, 1, 2, 13, 14])
STEP_SIZE = 0.02
DIFFUSE_FACTOR = 1.66
highest = lax.Precision.HIGHEST

def gll_tables():
    points = np.array([-1.0, -1.0 / np.sqrt(5.0), 1.0 / np.sqrt(5.0), 1.0])
    weights = np.array([1.0 / 6.0, 5.0 / 6.0, 5.0 / 6.0, 1.0 / 6.0])
    on_diag = np.eye(4, dtype=bool)
    diffs = np.where(on_diag, 1.0, points[:, None] - points[None, :])
    products = np.prod(diffs, axis=1)
    derivative = products[:, None] / products[None, :] / diffs
    inverse_diff = np.where(on_diag, 0.0, 1.0 / diffs)
    derivative = np.where(on_diag, inverse_diff.sum(axis=1)[:, None], derivative)
    second_diff = derivative @ derivative
    node_weight = weights[:, None] * weights[None, :]
    return (jnp.asarray(second_diff, jnp.float32), jnp.asarray(node_weight, jnp.float32))

def radiate(column_q, cos_zenith, albedo, absorb, rayleigh, solar):
    levels = column_q.shape[0]
    layer_tau = absorb.T[:, :, None] * (column_q * column_q)[:, None, :] + rayleigh[None, :, None]
    column_depth = jnp.cumsum(layer_tau, axis=0)
    top_flux = solar[:, None] * cos_zenith[None, :]
    direct_all = top_flux[None] * jnp.exp(-(column_depth - layer_tau) / cos_zenith[None, None, :])
    bottom_flux = top_flux * jnp.exp(-column_depth[-1] / cos_zenith[None, :])
    diffuse = jnp.exp(-DIFFUSE_FACTOR * layer_tau)
    reflect = 0.5 * (rayleigh[None, :, None] / layer_tau) * (1.0 - diffuse)

    def climb_up(below, layer):
        refl_now, diff_now = layer
        above = refl_now + diff_now * diff_now * below / (1.0 - refl_now * below)
        return (above, above)
    start_albedo = jnp.broadcast_to(albedo[None, :], top_flux.shape).astype(jnp.float32)
    _, level_albedo = lax.scan(climb_up, start_albedo, (reflect, diffuse), reverse=True)
    net_top = direct_all * (1.0 - level_albedo)
    net_bottom = bottom_flux * (1.0 - albedo[None, :])
    net_next = jnp.concatenate([net_top[1:], net_bottom[None]], axis=0)
    return levels * lax.optimization_barrier(jnp.sum(net_top - net_next, axis=1))

def radiate_blocks(column_q, cos_zenith, albedo, absorb, rayleigh, solar):
    levels, columns = column_q.shape
    block_size = min(columns, 512)
    block_count = columns // block_size
    q_blocks = column_q.reshape(levels, block_count, block_size).transpose(1, 0, 2)

    def one_block(block):
        return radiate(block[0], block[1], block[2], absorb, rayleigh, solar)
    results = lax.map(one_block, (q_blocks, cos_zenith.reshape(block_count, block_size), albedo.reshape(block_count, block_size)))
    return results.transpose(1, 0, 2).reshape(levels, columns)

def reference(moisture, jacobian, partners, daylit, cos_zenith, albedo, absorb, rayleigh, solar):
    levels = moisture.shape[0]
    elements = moisture.shape[2]
    second_diff, node_weight = gll_tables()
    nodal = moisture.reshape(levels, 4, 4, elements)
    second_x = jnp.einsum('ik,lkjn->lijn', second_diff, nodal, precision=highest)
    second_y = jnp.einsum('jk,likn->lijn', second_diff, nodal, precision=highest)
    weighted = (node_weight[None, :, :, None] * (second_x + second_y)).reshape(levels, 16, elements)
    masses = (node_weight[:, :, None] * jacobian[None, None, :]).reshape(16, elements)
    stacked = jnp.concatenate([weighted[:, edge_nodes, :], masses[edge_nodes][None]], axis=0)
    grouped = stacked.reshape(levels + 1, 8, N_GROUP, E_GROUP)
    west_side = jnp.roll(grouped[:, 2:4], 1, axis=3)
    east_side = jnp.roll(grouped[:, 0:2], -1, axis=3)
    local_partner = (partners % E_GROUP).reshape(2, N_GROUP, E_GROUP)
    south_index = jnp.broadcast_to(local_partner[0], (levels + 1, 2, N_GROUP, E_GROUP))
    north_index = jnp.broadcast_to(local_partner[1], (levels + 1, 2, N_GROUP, E_GROUP))
    south_side = jnp.take_along_axis(grouped[:, 4:6], south_index, axis=3)[:, ::-1]
    north_side = jnp.take_along_axis(grouped[:, 6:8], north_index, axis=3)[:, ::-1]
    partner_sum = jnp.concatenate([west_side, east_side, south_side, north_side], axis=1).reshape(levels + 1, 8, elements)
    assembled = stacked + partner_sum
    edge_ratio = assembled[:levels] / assembled[levels][None]
    tendency = weighted / masses[None]
    tendency = tendency.at[:, edge_nodes, :].set(edge_ratio)
    moisture_new = moisture + STEP_SIZE * tendency
    column_q = lax.optimization_barrier(jnp.sum(node_weight.reshape(16)[None, :, None] * moisture_new, axis=1)) / 4.0
    heat_all = radiate_blocks(column_q, cos_zenith, albedo, absorb, rayleigh, solar)
    heating = jnp.where(daylit[None, :] == 1, heat_all, jnp.float32(0.0))
    return (moisture_new, heating)
```

```python
import numpy as np
import jax
import jax.numpy as jnp
from jax import lax
from jax.experimental import pallas as pl
from jax.experimental.pallas import tpu as pltpu
from jax.sharding import PartitionSpec as P

LEV, G, E = 72, 112, 1024
HALF, LANES, GROUPS = E // 2, 128, LEV // 8
ROOT5 = float(np.sqrt(5.0))
STEP_SIZE = 0.02
CROSSED = (1, 2, 13, 14)
WEST, EAST = (4, 8), (7, 11)
J_ROW, PACK_ROW, SEND_ROWS = 288, 296, 304
G_BLOCKS = G // 8
EXPONENT = -1.66 * 1.4426950408889634


def second(v):
    mean = 1.25 * ((v[0] + v[3]) - (v[1] + v[2]))
    slope = 3.75 * ((v[0] - v[3]) - ROOT5 * (v[1] - v[2]))
    inner = slope * (1.0 / ROOT5)
    return (mean + slope, mean + inner, mean - inner, mean - slope)


def edge_values(m_ref, head_in, head_ref, tail_ref, tiles):
    group = pl.program_id(0)
    lane = lax.broadcasted_iota(jnp.int32, (8, LANES), 1)

    @pl.when(group == 0)
    def _():
        head_ref[J_ROW:J_ROW + 8] = jnp.broadcast_to(head_in[:, :HALF], (8, HALF))
        tail_ref[J_ROW:J_ROW + 8] = jnp.broadcast_to(head_in[:, HALF:], (8, HALF))
        head_ref[PACK_ROW:PACK_ROW + 8] = jnp.zeros((8, HALF), jnp.float32)
        tail_ref[PACK_ROW:PACK_ROW + 8] = jnp.zeros((8, HALF), jnp.float32)

    for block in range(E // LANES):
        cols = pl.ds(block * LANES, LANES)
        tiles[...] = m_ref[:, cols]
        node = {n: tiles[pl.ds(n, 8, stride=16), :] for n in range(16)}
        x_one = second([node[4 * k + 1] for k in range(4)])
        x_two = second([node[4 * k + 2] for k in range(4)])
        y_first = second([node[k] for k in range(4)])
        y_last = second([node[12 + k] for k in range(4)])
        values = (x_one[0] + y_first[1], x_two[0] + y_first[2], x_one[3] + y_last[1], x_two[3] + y_last[2])
        side, offset = (head_ref, block * LANES) if block * LANES < HALF else (tail_ref, block * LANES - HALF)
        for c, value in enumerate(values):
            rows = pl.ds(pl.multiple_of(c * LEV + group * 8, 8), 8)
            side[rows, pl.ds(offset, LANES)] = value
        for side, at, nodes, column, place in ((head_ref, 0, 0, 0, 0), (tail_ref, E // LANES - 1, 3, LANES - 1, 0)):
            if block != at:
                continue
            x_side = second([node[4 * k + nodes] for k in range(4)])
            y_one = second([node[4 + k] for k in range(4)])
            y_two = second([node[8 + k] for k in range(4)])
            packed = side[PACK_ROW:PACK_ROW + 8, :LANES]
            for a, value in enumerate((x_side[1] + y_one[nodes], x_side[2] + y_two[nodes])):
                spread = jnp.broadcast_to(value[:, column:column + 1], (8, LANES))
                packed = jnp.where(lane == a * GROUPS + group, spread, packed)
            side[PACK_ROW:PACK_ROW + 8, :LANES] = packed


def take_lanes(source, index):
    return jnp.take_along_axis(source, index, axis=1)


def assemble(m_ref, j_ref, partner_ref, head, tail, before, after, new_ref, q_ref, edge, scale, tiles, made):
    group = pl.program_id(0)
    lane = lax.broadcasted_iota(jnp.int32, (8, LANES), 1)
    blocks = E // LANES

    def crossing(side, rows_at, block):
        first, second_half = (before, head) if block < blocks // 2 else (tail, after)
        index = (partner_ref[side:side + 1, pl.ds(block * LANES, LANES)] + HALF) & (E - 1)
        index = jnp.broadcast_to(index, (8, LANES))
        inside, slot = index & (LANES - 1), index >> 7
        results = [None] * len(rows_at)
        for k in range(blocks):
            source = first if k < blocks // 2 else second_half
            here = slot == k
            for r, start in enumerate(rows_at):
                part = take_lanes(source[pl.ds(start, 8), pl.ds((k % (blocks // 2)) * LANES, LANES)], inside)
                results[r] = part if k == 0 else jnp.where(here, part, results[r])
        return results

    @pl.when(group == 0)
    def _():
        j_own = jnp.broadcast_to(j_ref[...], (8, E))
        for block in range(blocks):
            cols = pl.ds(block * LANES, LANES)
            own = j_own[:, block * LANES:(block + 1) * LANES]
            left = before[J_ROW:J_ROW + 8, HALF - LANES:] if block == 0 else j_own[:, (block - 1) * LANES:block * LANES]
            right = after[J_ROW:J_ROW + 8, :LANES] if block == blocks - 1 else j_own[:, (block + 1) * LANES:(block + 2) * LANES]
            west = jnp.where(lane == 0, pltpu.roll(left, 1, 1), pltpu.roll(own, 1, 1))
            east = jnp.where(lane == LANES - 1, pltpu.roll(right, LANES - 1, 1), pltpu.roll(own, LANES - 1, 1))
            south, = crossing(0, (J_ROW,), block)
            north, = crossing(1, (J_ROW,), block)
            scale[0, :, cols] = STEP_SIZE / own
            for s, other in enumerate((west, east, south, north)):
                scale[1 + s, :, cols] = STEP_SIZE / (own + other)

    for block in range(blocks):
        cols = pl.ds(block * LANES, LANES)
        tiles[block] = m_ref[:, cols]
        node = [tiles[block, pl.ds(n, 8, stride=16), :] for n in range(16)]
        along_x = [second([node[4 * k + j] for k in range(4)]) for j in range(4)]
        along_y = [second([node[4 * i + k] for k in range(4)]) for i in range(4)]
        inverse = scale[0, :, cols]
        corner, inner = 0.0, 0.0
        for n in range(16):
            i, j = n // 4, n % 4
            value = along_x[j][i] + along_y[i][j]
            ends = (i in (0, 3)) + (j in (0, 3))
            if ends == 1:
                edge[(WEST + EAST + CROSSED).index(n), :, cols] = value
                continue
            new = node[n] + inverse * value
            made[block, pl.ds(n, 8, stride=16), :] = new
            if ends == 2:
                corner = corner + new
            else:
                inner = inner + new
        q_ref[:, cols] = corner * (1.0 / 144.0) + inner * (25.0 / 144.0)

    packs = [
        [take_lanes(side[PACK_ROW:PACK_ROW + 8, :LANES], jnp.zeros((8, LANES), jnp.int32) + (a * GROUPS + group)) for a in range(2)]
        for side in (before, after)
    ]
    starts = [pl.multiple_of(c * LEV + group * 8, 8) for c in range(4)]
    for block in range(blocks):
        cols = pl.ds(block * LANES, LANES)
        others = []
        for a in range(2):
            own = edge[2 + a, :, cols]
            carried = packs[0][a] if block == 0 else pltpu.roll(edge[2 + a, :, pl.ds((block - 1) * LANES, LANES)], 1, 1)
            others.append(jnp.where(lane == 0, carried, pltpu.roll(own, 1, 1)))
        for a in range(2):
            own = edge[a, :, cols]
            if block == blocks - 1:
                carried = packs[1][a]
            else:
                carried = pltpu.roll(edge[a, :, pl.ds((block + 1) * LANES, LANES)], LANES - 1, 1)
            others.append(jnp.where(lane == LANES - 1, carried, pltpu.roll(own, LANES - 1, 1)))
        others += crossing(0, (starts[1], starts[0]), block)
        others += crossing(1, (starts[3], starts[2]), block)
        total = 0.0
        for k, n in enumerate(WEST + EAST + CROSSED):
            value = edge[k, :, cols] + others[k]
            new = tiles[block, pl.ds(n, 8, stride=16), :] + scale[1 + k // 2, :, cols] * value
            made[block, pl.ds(n, 8, stride=16), :] = new
            total = total + new
        q_ref[:, cols] += total * (5.0 / 144.0)
        new_ref[:, cols] = made[block]


def radiate(q_ref, mu_ref, alb_ref, lit_ref, absorb_ref, ray_ref, solar_ref, out_ref, absb, rayb, solb, flux, partial, q_wide):
    scaled = absorb_ref[...] * EXPONENT
    for level in range(LEV):
        absb[level] = jnp.broadcast_to(scaled[:, level:level + 1], (G, LANES)).reshape(G_BLOCKS, 8, LANES)
    rayb[...] = jnp.broadcast_to(ray_ref[...] * EXPONENT, (G, LANES)).reshape(G_BLOCKS, 8, LANES)
    solb[...] = jnp.broadcast_to(solar_ref[...], (G, LANES)).reshape(G_BLOCKS, 8, LANES)

    def one_block(block, carry):
        cols = pl.ds(pl.multiple_of(block * LANES, LANES), LANES)
        lit = lit_ref[0:1, cols]
        count = jnp.sum(lit)

        @pl.when(count == 0)
        def _():
            out_ref[:, cols] = jnp.zeros((LEV, LANES), jnp.float32)

        @pl.when(count > 0)
        def _():
            mu = mu_ref[0:1, cols]
            alb = alb_ref[0:1, cols]
            slant = jnp.broadcast_to(1.0 / (1.66 * mu), (8, LANES))
            square = q_ref[:, cols]
            square = square * square
            for level in range(LEV):
                q_wide[level] = jnp.broadcast_to(square[level:level + 1], (8, LANES))

            def down(level, direct):
                flux[level] = direct
                depth = absb[level] * q_wide[level][None] + rayb[...]
                return direct * jnp.exp2(depth * slant[None])

            direct = lax.fori_loop(0, LEV, down, solb[...], unroll=4)
            partial[LEV] = jnp.sum(direct * (1.0 - alb)[None], axis=0)

            def up(step, below):
                level = LEV - 1 - step
                ray = rayb[...]
                depth = absb[level] * q_wide[level][None] + ray
                diffuse = jnp.exp2(depth)
                half = ray * 0.5
                rho = half - half * diffuse
                rest = depth - rho * below
                through = diffuse * depth
                above = (rho * rest + through * through * below) / (depth * rest)
                partial[level] = jnp.sum(flux[level] * (1.0 - above), axis=0)
                return above

            lax.fori_loop(0, LEV, up, jnp.broadcast_to(alb[None], (G_BLOCKS, 8, LANES)), unroll=4)
            net = jnp.sum(partial[...], axis=1)
            heat = (net[:LEV] - net[1:LEV + 1]) * (72.0 * mu)
            out_ref[:, cols] = jnp.where(lit == 1, heat, 0.0)

        return carry

    lax.fori_loop(0, E // LANES, one_block, 0)


def whole(shape):
    return pl.BlockSpec(shape, lambda g: (0,) * len(shape))


def shards(moisture, jacobian, partners, daylit, cos_zenith, albedo, absorb, rayleigh, solar):
    f32 = jnp.float32
    flat = moisture.reshape(LEV * 16, E)
    jac = jacobian.reshape(1, E)
    rows = pl.BlockSpec((128, E), lambda g: (g, 0))
    head, tail = pl.pallas_call(
        edge_values,
        grid=(GROUPS,),
        in_specs=[rows, whole((1, E))],
        out_specs=[whole((SEND_ROWS, HALF))] * 2,
        out_shape=[jax.ShapeDtypeStruct((SEND_ROWS, HALF), f32)] * 2,
        scratch_shapes=[pltpu.VMEM((128, LANES), f32)],
        name="edge_values",
    )(flat, jac)
    count = lax.axis_size("curve")
    before = lax.ppermute(tail, "curve", [(i, (i + 1) % count) for i in range(count)])
    after = lax.ppermute(head, "curve", [((i + 1) % count, i) for i in range(count)])
    new, column_q = pl.pallas_call(
        assemble,
        grid=(GROUPS,),
        in_specs=[rows, whole((1, E)), whole((2, E))] + [whole((SEND_ROWS, HALF))] * 4,
        out_specs=[rows, pl.BlockSpec((8, E), lambda g: (g, 0))],
        out_shape=[jax.ShapeDtypeStruct((LEV * 16, E), f32), jax.ShapeDtypeStruct((LEV, E), f32)],
        scratch_shapes=[
            pltpu.VMEM((8, 8, E), f32),
            pltpu.VMEM((5, 8, E), f32),
            pltpu.VMEM((8, 128, LANES), f32),
            pltpu.VMEM((8, 128, LANES), f32),
        ],
        name="assemble",
    )(flat, jac, partners, head, tail, before, after)
    heating = pl.pallas_call(
        radiate,
        in_specs=[pl.BlockSpec(memory_space=pltpu.VMEM)] * 7,
        out_specs=pl.BlockSpec(memory_space=pltpu.VMEM),
        out_shape=jax.ShapeDtypeStruct((LEV, E), f32),
        scratch_shapes=[
            pltpu.VMEM((LEV, G_BLOCKS, 8, LANES), f32),
            pltpu.VMEM((G_BLOCKS, 8, LANES), f32),
            pltpu.VMEM((G_BLOCKS, 8, LANES), f32),
            pltpu.VMEM((LEV, G_BLOCKS, 8, LANES), f32),
            pltpu.VMEM((LEV + 1, 8, LANES), f32),
            pltpu.VMEM((LEV, 8, LANES), f32),
        ],
        compiler_params=pltpu.CompilerParams(vmem_limit_bytes=48 * 2**20),
        name="radiate",
    )(
        column_q,
        cos_zenith.reshape(1, E),
        albedo.reshape(1, E),
        daylit.reshape(1, E),
        absorb,
        rayleigh.reshape(G, 1),
        solar.reshape(G, 1),
    )
    return (new.reshape(LEV, 16, E), heating)


def solution(mesh):
    columns = P(("group", "curve"))
    placed = (
        P(None, None, ("group", "curve")),
        columns,
        P(None, ("group", "curve")),
        columns,
        columns,
        columns,
        P(),
        P(),
        P(),
    )
    return jax.shard_map(
        shards,
        mesh=mesh,
        in_specs=placed,
        out_specs=(P(None, None, ("group", "curve")), P(None, ("group", "curve"))),
        check_vma=False,
    )
```

```python
import numpy as np
import jax
import jax.numpy as jnp
from jax import lax
from jax.experimental import pallas as pl
from jax.experimental.pallas import tpu as pltpu
from jax.sharding import PartitionSpec as P

LEV, G, E = 72, 112, 1024
HALF, LANES, GROUPS = E // 2, 128, LEV // 8
ROOT5 = float(np.sqrt(5.0))
STEP_SIZE = 0.02
CROSSED = (1, 2, 13, 14)
SIDES = (4, 8, 7, 11)
G_BLOCKS = G // 8
EXPONENT = -1.66 * 1.4426950408889634


def second(v):
    mean = 1.25 * ((v[0] + v[3]) - (v[1] + v[2]))
    slope = 3.75 * ((v[0] - v[3]) - ROOT5 * (v[1] - v[2]))
    inner = slope * (1.0 / ROOT5)
    return (mean + slope, mean + inner, mean - inner, mean - slope)


def take_lanes(source, index):
    return jnp.take_along_axis(source, index, axis=1)


def exchange(
    m_hbm, j_hbm, partner_hbm, new_hbm, q_ref, held, made, sides, crossed, jac, scale, inside, slot,
    j_ref, partner_ref, in_sem, out_sem, send_sem, recv_sem,
):
    me = lax.axis_index("curve")
    count = lax.axis_size("curve")
    right, left = lax.rem(me + 1, count), lax.rem(me + count - 1, count)
    blocks = E // LANES
    lane = lax.broadcasted_iota(jnp.int32, (8, LANES), 1)

    def fetch(group):
        rows = pl.ds(pl.multiple_of(group * 128, 128), 128)
        return pltpu.make_async_copy(m_hbm.at[rows], held.at[group], in_sem.at[group])

    def deliver(group):
        rows = pl.ds(pl.multiple_of(group * 128, 128), 128)
        return pltpu.make_async_copy(held.at[group], new_hbm.at[rows], out_sem.at[group])

    def send(way, group):
        return pltpu.make_async_remote_copy(
            src_ref=crossed.at[group, 2 - way],
            dst_ref=crossed.at[group, 3 * way],
            send_sem=send_sem.at[way, group],
            recv_sem=recv_sem.at[way, group],
            device_id={"curve": left if way else right},
            device_id_type=pl.DeviceIdType.MESH,
        )

    def send_jacobian(way):
        return pltpu.make_async_remote_copy(
            src_ref=jac.at[pl.ds(4 if way else 8, 4)],
            dst_ref=jac.at[pl.ds(12 if way else 0, 4)],
            send_sem=send_sem.at[way, GROUPS],
            recv_sem=recv_sem.at[way, GROUPS],
            device_id={"curve": left if way else right},
            device_id_type=pl.DeviceIdType.MESH,
        )

    barrier = pltpu.get_barrier_semaphore()
    for neighbour in (left, right):
        pl.semaphore_signal(barrier, inc=1, device_id={"curve": neighbour}, device_id_type=pl.DeviceIdType.MESH)
    small = [
        pltpu.make_async_copy(j_hbm, j_ref, in_sem.at[GROUPS]),
        pltpu.make_async_copy(partner_hbm, partner_ref, in_sem.at[GROUPS + 1]),
    ]
    for copy in small:
        copy.start()
    for group in range(GROUPS):
        fetch(group).start()
    for copy in small:
        copy.wait()
    for block in range(blocks):
        cols = pl.ds(block * LANES, LANES)
        own = jnp.broadcast_to(j_ref[:, cols], (8, LANES))
        jac[4 + block] = own
        scale[0, block] = STEP_SIZE / own
        for side in range(2):
            index = (jnp.broadcast_to(partner_ref[side:side + 1, cols], (8, LANES)) + HALF) & (E - 1)
            inside[side, block] = index & (LANES - 1)
            slot[side, block] = index >> 7
    pl.semaphore_wait(barrier, 2)
    for way in range(2):
        send_jacobian(way).start()

    def first_part(group, carry):
        fetch(group).wait()
        for block in range(blocks):
            cols = pl.ds(block * LANES, LANES)
            made[group, block] = held[group, :, cols]
            node = [made[group, block, pl.ds(n, 8, stride=16), :] for n in range(16)]
            along_x = [second([node[4 * k + j] for k in range(4)]) for j in range(4)]
            along_y = [second([node[4 * i + k] for k in range(4)]) for i in range(4)]
            inverse = scale[0, block]
            corner, inner = 0.0, 0.0
            section, place = 1 + block // 4, (block % 4) * 4
            for n in range(16):
                i, j = n // 4, n % 4
                value = along_x[j][i] + along_y[i][j]
                if n in CROSSED:
                    crossed[group, section, place + CROSSED.index(n)] = value
                    continue
                if n in SIDES:
                    k = SIDES.index(n)
                    sides[group, k, block] = value
                    if block == 0 and k < 2:
                        crossed[group, 1, 16 + k] = value
                    if block == blocks - 1 and k >= 2:
                        crossed[group, 2, 16 + k - 2] = value
                    continue
                new = node[n] + inverse * value
                made[group, block, pl.ds(n, 8, stride=16), :] = new
                if i in (0, 3):
                    corner = corner + new
                else:
                    inner = inner + new
            q_ref[pl.ds(pl.multiple_of(group * 8, 8), 8), cols] = corner * (1.0 / 144.0) + inner * (25.0 / 144.0)
        for way in range(2):
            send(way, group).start()
        return carry

    lax.fori_loop(0, GROUPS, first_part, 0)

    def gather(side, block, window):
        where, which = inside[side, block], slot[side, block]
        results = None
        for k in range(blocks):
            parts = [take_lanes(source, where) for source in window(k)]
            here = which == k
            results = parts if k == 0 else [jnp.where(here, p, r) for p, r in zip(parts, results)]
        return results

    for way in range(2):
        send_jacobian(way).wait()
    for block in range(blocks):
        own = jac[4 + block]
        west = jnp.where(lane == 0, pltpu.roll(jac[3 + block], 1, 1), pltpu.roll(own, 1, 1))
        east = jnp.where(lane == LANES - 1, pltpu.roll(jac[5 + block], LANES - 1, 1), pltpu.roll(own, LANES - 1, 1))
        base = 8 * (block // 4)
        south, = gather(0, block, lambda k: [jac[base + k]])
        north, = gather(1, block, lambda k: [jac[base + k]])
        for s, other in enumerate((west, east, south, north)):
            scale[1 + s, block] = STEP_SIZE / (own + other)

    def second_part(group, carry):
        for way in range(2):
            send(way, group).wait()
        for block in range(blocks):
            cols = pl.ds(block * LANES, LANES)
            section, place = 1 + block // 4, (block % 4) * 4
            others = []
            for a in range(2):
                last = crossed[group, 0, 16 + a] if block == 0 else sides[group, 2 + a, block - 1]
                others.append(jnp.where(lane == 0, pltpu.roll(last, 1, 1), pltpu.roll(sides[group, 2 + a, block], 1, 1)))
            for a in range(2):
                following = crossed[group, 3, 16 + a] if block == blocks - 1 else sides[group, a, block + 1]
                others.append(
                    jnp.where(lane == LANES - 1, pltpu.roll(following, LANES - 1, 1), pltpu.roll(sides[group, a, block], LANES - 1, 1))
                )
            for side in range(2):
                def window(k):
                    return [crossed[group, 2 * (block // 4) + k // 4, (k % 4) * 4 + 2 * side + c] for c in (1, 0)]
                others += gather(side, block, window)
            total = 0.0
            for k, n in enumerate(SIDES + CROSSED):
                own = sides[group, k, block] if k < 4 else crossed[group, section, place + k - 4]
                new = made[group, block, pl.ds(n, 8, stride=16), :] + scale[1 + k // 2, block] * (own + others[k])
                made[group, block, pl.ds(n, 8, stride=16), :] = new
                total = total + new
            q_ref[pl.ds(pl.multiple_of(group * 8, 8), 8), cols] += total * (5.0 / 144.0)
            held[group, :, cols] = made[group, block]
        deliver(group).start()
        return carry

    lax.fori_loop(0, GROUPS, second_part, 0)

    def finish(group, carry):
        deliver(group).wait()
        return carry

    lax.fori_loop(0, GROUPS, finish, 0)


def radiate(q_hbm, mu_ref, alb_ref, lit_ref, absorb_ref, ray_ref, solar_ref, new_ref, out_ref, kept_ref, absb, rayb, solb, flux, partial, q_wide, q_ref, kept_sem, q_sem):
    fetch = pltpu.make_async_copy(q_hbm, q_ref, q_sem)
    fetch.start()
    keep = pltpu.make_async_copy(new_ref, kept_ref, kept_sem)
    keep.start()
    scaled = absorb_ref[...].T * EXPONENT
    for level in range(LEV):
        absb[level] = jnp.broadcast_to(scaled[:, level:level + 1], (G, LANES)).reshape(G_BLOCKS, 8, LANES)
    rayb[...] = jnp.broadcast_to(ray_ref[...].T * EXPONENT, (G, LANES)).reshape(G_BLOCKS, 8, LANES)
    solb[...] = jnp.broadcast_to(solar_ref[...].T, (G, LANES)).reshape(G_BLOCKS, 8, LANES)

    fetch.wait()

    def one_block(block, carry):
        cols = pl.ds(pl.multiple_of(block * LANES, LANES), LANES)
        lit = lit_ref[0:1, cols]
        count = jnp.sum(lit)

        @pl.when(count == 0)
        def _():
            out_ref[:, cols] = jnp.zeros((LEV, LANES), jnp.float32)

        @pl.when(count > 0)
        def _():
            mu = mu_ref[0:1, cols]
            alb = alb_ref[0:1, cols]
            slant = jnp.broadcast_to(1.0 / (1.66 * mu), (8, LANES))
            square = q_ref[:, cols]
            square = square * square
            for level in range(LEV):
                q_wide[level] = jnp.broadcast_to(square[level:level + 1], (8, LANES))

            def down(level, direct):
                flux[level] = direct
                depth = absb[level] * q_wide[level][None] + rayb[...]
                return direct * jnp.exp2(depth * slant[None])

            direct = lax.fori_loop(0, LEV, down, solb[...], unroll=4)
            partial[LEV] = jnp.sum(direct * (1.0 - alb)[None], axis=0)

            def up(step, below):
                level = LEV - 1 - step
                ray = rayb[...]
                depth = absb[level] * q_wide[level][None] + ray
                diffuse = jnp.exp2(depth)
                half = ray * 0.5
                rho = half - half * diffuse
                rest = depth - rho * below
                through = diffuse * depth
                above = (rho * rest + through * through * below) / (depth * rest)
                partial[level] = jnp.sum(flux[level] * (1.0 - above), axis=0)
                return above

            lax.fori_loop(0, LEV, up, jnp.broadcast_to(alb[None], (G_BLOCKS, 8, LANES)), unroll=4)
            net = jnp.sum(partial[...], axis=1)
            heat = (net[:LEV] - net[1:LEV + 1]) * (72.0 * mu)
            out_ref[:, cols] = jnp.where(lit == 1, heat, 0.0)

        return carry

    lax.fori_loop(0, E // LANES, one_block, 0)
    keep.wait()


def shards(moisture, jacobian, partners, daylit, cos_zenith, albedo, absorb, rayleigh, solar):
    f32 = jnp.float32
    flat = moisture.reshape(LEV * 16, E)
    jac = jacobian.reshape(1, E)
    vmem, anywhere = pl.BlockSpec(memory_space=pltpu.VMEM), pl.BlockSpec(memory_space=pl.ANY)
    tile = (8, LANES)
    new, column_q = pl.pallas_call(
        exchange,
        in_specs=[anywhere] * 3,
        out_specs=[anywhere, vmem],
        out_shape=[jax.ShapeDtypeStruct((LEV * 16, E), f32), jax.ShapeDtypeStruct((LEV, E), f32)],
        scratch_shapes=[
            pltpu.VMEM((GROUPS, 128, E), f32),
            pltpu.VMEM((GROUPS, 8, 128, LANES), f32),
            pltpu.VMEM((GROUPS, 4, 8) + tile, f32),
            pltpu.VMEM((GROUPS, 4, 18) + tile, f32),
            pltpu.VMEM((16,) + tile, f32),
            pltpu.VMEM((5, 8) + tile, f32),
            pltpu.VMEM((2, 8) + tile, jnp.int32),
            pltpu.VMEM((2, 8) + tile, jnp.int32),
            pltpu.VMEM((1, E), f32),
            pltpu.VMEM((2, E), jnp.int32),
            pltpu.SemaphoreType.DMA((GROUPS + 2,)),
            pltpu.SemaphoreType.DMA((GROUPS,)),
            pltpu.SemaphoreType.DMA((2, GROUPS + 1)),
            pltpu.SemaphoreType.DMA((2, GROUPS + 1)),
        ],
        compiler_params=pltpu.CompilerParams(collective_id=0, has_side_effects=True, vmem_limit_bytes=60 * 2**20),
        name="exchange",
    )(flat, jac, partners)
    heating, new = pl.pallas_call(
        radiate,
        in_specs=[anywhere] + [vmem] * 6 + [anywhere],
        out_specs=[vmem, anywhere],
        out_shape=[jax.ShapeDtypeStruct((LEV, E), f32), jax.ShapeDtypeStruct((LEV * 16, E), f32)],
        scratch_shapes=[
            pltpu.VMEM((LEV, G_BLOCKS, 8, LANES), f32),
            pltpu.VMEM((G_BLOCKS, 8, LANES), f32),
            pltpu.VMEM((G_BLOCKS, 8, LANES), f32),
            pltpu.VMEM((LEV, G_BLOCKS, 8, LANES), f32),
            pltpu.VMEM((LEV + 1, 8, LANES), f32),
            pltpu.VMEM((LEV, 8, LANES), f32),
            pltpu.VMEM((LEV, E), f32),
            pltpu.SemaphoreType.DMA,
            pltpu.SemaphoreType.DMA,
        ],
        compiler_params=pltpu.CompilerParams(vmem_limit_bytes=60 * 2**20),
        name="radiate",
    )(
        column_q,
        cos_zenith.reshape(1, E),
        albedo.reshape(1, E),
        daylit.reshape(1, E),
        absorb.T,
        rayleigh.reshape(1, G),
        solar.reshape(1, G),
        new,
    )
    return (new.reshape(LEV, 16, E), heating)


def solution(mesh):
    columns = P(("group", "curve"))
    placed = (
        P(None, None, ("group", "curve")),
        columns,
        P(None, ("group", "curve")),
        columns,
        columns,
        columns,
        P(),
        P(),
        P(),
    )
    return jax.shard_map(
        shards,
        mesh=mesh,
        in_specs=placed,
        out_specs=(P(None, None, ("group", "curve")), P(None, ("group", "curve"))),
        check_vma=False,
    )
```

```python
import numpy as np
import jax
import jax.numpy as jnp
from jax import lax
from jax.experimental import pallas as pl
from jax.experimental.pallas import tpu as pltpu
from jax.sharding import PartitionSpec as P

LEV, G, E = 72, 112, 1024
HALF, LANES, GROUPS = E // 2, 128, LEV // 8
ROOT5 = float(np.sqrt(5.0))
STEP_SIZE = 0.02
CROSSED = (1, 2, 13, 14)
SIDES = (4, 8, 7, 11)
G_BLOCKS = G // 8
CHAINS = G_BLOCKS // 2
STEP = 8
STEPS = LEV // STEP
RAYS = 4
EXPONENT = -1.66 * 1.4426950408889634


def second(v):
    mean = 1.25 * ((v[0] + v[3]) - (v[1] + v[2]))
    slope = 3.75 * ((v[0] - v[3]) - ROOT5 * (v[1] - v[2]))
    inner = slope * (1.0 / ROOT5)
    return (mean + slope, mean + inner, mean - inner, mean - slope)


def take_lanes(source, index):
    return jnp.take_along_axis(source, index, axis=1)


def exchange(
    m_hbm, j_hbm, partner_hbm, new_hbm, q_ref, held, made, sides, crossed, jac, scale, inside, slot,
    j_ref, partner_ref, in_sem, out_sem, send_sem, recv_sem,
):
    me = lax.axis_index("curve")
    count = lax.axis_size("curve")
    right, left = lax.rem(me + 1, count), lax.rem(me + count - 1, count)
    blocks = E // LANES
    lane = lax.broadcasted_iota(jnp.int32, (8, LANES), 1)

    def fetch(group):
        rows = pl.ds(pl.multiple_of(group * 128, 128), 128)
        return pltpu.make_async_copy(m_hbm.at[rows], held.at[group], in_sem.at[group])

    def deliver(group):
        rows = pl.ds(pl.multiple_of(group * 128, 128), 128)
        return pltpu.make_async_copy(held.at[group], new_hbm.at[rows], out_sem.at[group])

    def send(way, group):
        return pltpu.make_async_remote_copy(
            src_ref=crossed.at[group, 2 - way],
            dst_ref=crossed.at[group, 3 * way],
            send_sem=send_sem.at[way, group],
            recv_sem=recv_sem.at[way, group],
            device_id={"curve": left if way else right},
            device_id_type=pl.DeviceIdType.MESH,
        )

    def send_jacobian(way):
        return pltpu.make_async_remote_copy(
            src_ref=jac.at[pl.ds(4 if way else 8, 4)],
            dst_ref=jac.at[pl.ds(12 if way else 0, 4)],
            send_sem=send_sem.at[way, GROUPS],
            recv_sem=recv_sem.at[way, GROUPS],
            device_id={"curve": left if way else right},
            device_id_type=pl.DeviceIdType.MESH,
        )

    barrier = pltpu.get_barrier_semaphore()
    for neighbour in (left, right):
        pl.semaphore_signal(barrier, inc=1, device_id={"curve": neighbour}, device_id_type=pl.DeviceIdType.MESH)
    small = [
        pltpu.make_async_copy(j_hbm, j_ref, in_sem.at[GROUPS]),
        pltpu.make_async_copy(partner_hbm, partner_ref, in_sem.at[GROUPS + 1]),
    ]
    for copy in small:
        copy.start()
    for group in range(GROUPS):
        fetch(group).start()
    for copy in small:
        copy.wait()
    for block in range(blocks):
        cols = pl.ds(block * LANES, LANES)
        own = jnp.broadcast_to(j_ref[:, cols], (8, LANES))
        jac[4 + block] = own
        scale[0, block] = STEP_SIZE / own
        for side in range(2):
            index = (jnp.broadcast_to(partner_ref[side:side + 1, cols], (8, LANES)) + HALF) & (E - 1)
            inside[side, block] = index & (LANES - 1)
            slot[side, block] = index >> 7
    pl.semaphore_wait(barrier, 2)
    for way in range(2):
        send_jacobian(way).start()

    def first_part(group, carry):
        fetch(group).wait()
        for block in range(blocks):
            cols = pl.ds(block * LANES, LANES)
            made[group, block] = held[group, :, cols]
            node = [made[group, block, pl.ds(n, 8, stride=16), :] for n in range(16)]
            along_x = [second([node[4 * k + j] for k in range(4)]) for j in range(4)]
            along_y = [second([node[4 * i + k] for k in range(4)]) for i in range(4)]
            inverse = scale[0, block]
            corner, inner = 0.0, 0.0
            section, place = 1 + block // 4, (block % 4) * 4
            for n in range(16):
                i, j = n // 4, n % 4
                value = along_x[j][i] + along_y[i][j]
                if n in CROSSED:
                    crossed[group, section, place + CROSSED.index(n)] = value
                    continue
                if n in SIDES:
                    k = SIDES.index(n)
                    sides[group, k, block] = value
                    if block == 0 and k < 2:
                        crossed[group, 1, 16 + k] = value
                    if block == blocks - 1 and k >= 2:
                        crossed[group, 2, 16 + k - 2] = value
                    continue
                new = node[n] + inverse * value
                made[group, block, pl.ds(n, 8, stride=16), :] = new
                if i in (0, 3):
                    corner = corner + new
                else:
                    inner = inner + new
            q_ref[pl.ds(pl.multiple_of(group * 8, 8), 8), cols] = corner * (1.0 / 144.0) + inner * (25.0 / 144.0)
        for way in range(2):
            send(way, group).start()
        return carry

    lax.fori_loop(0, GROUPS, first_part, 0)

    def gather(side, block, window):
        where, which = inside[side, block], slot[side, block]
        results = None
        for k in range(blocks):
            parts = [take_lanes(source, where) for source in window(k)]
            here = which == k
            results = parts if k == 0 else [jnp.where(here, p, r) for p, r in zip(parts, results)]
        return results

    for way in range(2):
        send_jacobian(way).wait()
    for block in range(blocks):
        own = jac[4 + block]
        west = jnp.where(lane == 0, pltpu.roll(jac[3 + block], 1, 1), pltpu.roll(own, 1, 1))
        east = jnp.where(lane == LANES - 1, pltpu.roll(jac[5 + block], LANES - 1, 1), pltpu.roll(own, LANES - 1, 1))
        base = 8 * (block // 4)
        south, = gather(0, block, lambda k: [jac[base + k]])
        north, = gather(1, block, lambda k: [jac[base + k]])
        for s, other in enumerate((west, east, south, north)):
            scale[1 + s, block] = STEP_SIZE / (own + other)

    def second_part(group, carry):
        for way in range(2):
            send(way, group).wait()
        for block in range(blocks):
            cols = pl.ds(block * LANES, LANES)
            section, place = 1 + block // 4, (block % 4) * 4
            others = []
            for a in range(2):
                last = crossed[group, 0, 16 + a] if block == 0 else sides[group, 2 + a, block - 1]
                others.append(jnp.where(lane == 0, pltpu.roll(last, 1, 1), pltpu.roll(sides[group, 2 + a, block], 1, 1)))
            for a in range(2):
                following = crossed[group, 3, 16 + a] if block == blocks - 1 else sides[group, a, block + 1]
                others.append(
                    jnp.where(lane == LANES - 1, pltpu.roll(following, LANES - 1, 1), pltpu.roll(sides[group, a, block], LANES - 1, 1))
                )
            for side in range(2):
                def window(k):
                    return [crossed[group, 2 * (block // 4) + k // 4, (k % 4) * 4 + 2 * side + c] for c in (1, 0)]
                others += gather(side, block, window)
            total = 0.0
            for k, n in enumerate(SIDES + CROSSED):
                own = sides[group, k, block] if k < 4 else crossed[group, section, place + k - 4]
                new = made[group, block, pl.ds(n, 8, stride=16), :] + scale[1 + k // 2, block] * (own + others[k])
                made[group, block, pl.ds(n, 8, stride=16), :] = new
                total = total + new
            q_ref[pl.ds(pl.multiple_of(group * 8, 8), 8), cols] += total * (5.0 / 144.0)
            held[group, :, cols] = made[group, block]
        deliver(group).start()
        return carry

    lax.fori_loop(0, GROUPS, second_part, 0)

    def finish(group, carry):
        deliver(group).wait()
        return carry

    lax.fori_loop(0, GROUPS, finish, 0)


def summands(x, count):
    parts = []
    for _ in range(count):
        parts.append(x.astype(jnp.bfloat16).astype(jnp.float32))
        x = x - parts[-1]
    return parts


def short_summands(x, count):
    parts = []
    for _ in range(count):
        big = x * float(2**20 + 1)
        parts.append(big - (big - x))
        x = x - parts[-1]
    return parts


def build_left(left, absorb, ray, solar):
    high, low = summands(absorb, 2)
    rays = short_summands(ray, RAYS)
    logs = summands(jnp.log2(solar), 3)
    used = 3 * LEV + 2 * RAYS + 6
    source = jnp.concatenate(
        [high, high, low] + rays + rays + [logs[0], logs[0], logs[1], logs[1], logs[2], logs[0]]
        + [jnp.zeros((G, 256 - used), jnp.float32)],
        axis=1,
    ).astype(jnp.bfloat16)
    column = lax.broadcasted_iota(jnp.int32, (1, 256), 1)
    level_of = jnp.where(column < LEV, column, jnp.where(column < 2 * LEV, column - LEV, column - 2 * LEV))
    absorbs = column < 3 * LEV
    eights = (column >= 3 * LEV) & (column < 3 * LEV + RAYS)
    ones = (column >= 3 * LEV + RAYS) & (column < 3 * LEV + 2 * RAYS)
    for level in range(LEV):
        step, i = divmod(LEV - 1 - level, STEP)
        single = jnp.where(absorbs, (level_of == level).astype(jnp.float32), jnp.where(ones, 1.0, 0.0))
        tens, units = divmod(level + 1, 8)
        rest = jnp.where(eights, float(tens), jnp.where(ones, float(units), 1.0))
        summed = jnp.where(absorbs, (level_of <= level).astype(jnp.float32), rest)
        for kind, mask in enumerate((single, summed)):
            rows = pl.ds((kind * STEP + i) * G, G)
            left[step, rows, :] = source * jnp.broadcast_to(mask, (G, 256)).astype(jnp.bfloat16)


def build_right(q, mu):
    high, low = summands(q * q, 2)
    cos = summands(1.66 * mu, 3)
    one = jnp.ones((RAYS, LANES), jnp.float32)
    used = 3 * LEV + 2 * RAYS + 6
    rows = [high, low, high, one * 8.0, one, cos[0], cos[1], cos[0], cos[1], cos[0], cos[2]]
    return jnp.concatenate(rows + [jnp.zeros((256 - used, LANES), jnp.float32)], axis=0).astype(jnp.bfloat16)


def radiate(
    q_hbm, mu_ref, alb_ref, lit_ref, absorb_ref, ray_ref, solar_ref, new_hbm, out_ref, kept_hbm,
    left, right, half_ray, top, even, odd, climbing, net, q_ref, new_ref, q_sem, new_sem, kept_sem,
):
    fetch = pltpu.make_async_copy(q_hbm, q_ref, q_sem)
    land = pltpu.make_async_copy(new_hbm, new_ref, new_sem)
    keep = pltpu.make_async_copy(new_ref, kept_hbm, kept_sem)
    fetch.start()
    land.start()
    lit_count = jnp.sum(lit_ref[...])
    pairs = E // (2 * LANES)

    @pl.when(lit_count > 0)
    def _():
        ray = ray_ref[...].T * EXPONENT
        solar = solar_ref[...].T
        build_left(left, absorb_ref[...].T * EXPONENT, ray, solar)
        half_ray[...] = jnp.broadcast_to(ray * 0.5, (G, LANES)).reshape(G_BLOCKS, 8, LANES)
        top[...] = jnp.broadcast_to(solar, (G, LANES)).reshape(G_BLOCKS, 8, LANES)

    fetch.wait()
    land.wait()
    keep.start()

    def columns(pair, b):
        return pl.ds(pl.multiple_of((2 * pair + b) * LANES, LANES), LANES)

    def depths(n, buffer):
        pair, step = lax.div(n, STEPS), lax.rem(n, STEPS)
        buffer[...] = jnp.dot(left[step], right[pair], preferred_element_type=jnp.float32)

    def climb(n, buffer, following, next_buffer):
        pair, step = lax.div(n, STEPS), lax.rem(n, STEPS)

        @pl.when(step == 0)
        def _():
            for b in range(2):
                climbing[b] = jnp.broadcast_to(alb_ref[0:1, columns(pair, b)][None], (G_BLOCKS, 8, LANES))

        totals = {}
        for b in range(2):
            lanes = slice(b * LANES, (b + 1) * LANES)
            slant = jnp.broadcast_to(1.0 / (1.66 * mu_ref[0:1, columns(pair, b)]), (8, LANES))[None]
            for half in range(2):
                chains = pl.ds(half * CHAINS, CHAINS)
                below = climbing[b, chains]
                ray = half_ray[chains]
                for i in range(STEP):
                    level = LEV - 1 - step * STEP - i
                    first = i * G + half * CHAINS * 8
                    second_kind = first + STEP * G
                    depth = buffer[first:first + CHAINS * 8, lanes].reshape(CHAINS, 8, LANES)
                    above_it = buffer[second_kind:second_kind + CHAINS * 8, lanes].reshape(CHAINS, 8, LANES)
                    totals[half, i] = jnp.sum(jnp.exp2(above_it * slant) * (1.0 - below), axis=0)
                    if half == 1:
                        net[b, level + 1] = totals[0, i] + totals[1, i]
                    diffuse = jnp.exp2(depth)
                    reflect = (ray - ray * diffuse) * (1.0 / depth)
                    below = reflect + diffuse * diffuse * below * (1.0 / (1.0 - reflect * below))
                climbing[b, chains] = below
        depths(following, next_buffer)

        @pl.when(step == STEPS - 1)
        def _():
            for b in range(2):
                cols = columns(pair, b)
                net[b, 0] = jnp.sum(top[...] * (1.0 - climbing[b]), axis=0)
                total = jnp.sum(net[b], axis=1)
                heat = (total[:LEV] - total[1:]) * (72.0 * mu_ref[0:1, cols])
                out_ref[:, cols] = jnp.where(lit_ref[0:1, cols] == 1, heat, 0.0)

    @pl.when(lit_count > 0)
    def _():
        for pair in range(pairs):
            for b in range(2):
                cols = slice((2 * pair + b) * LANES, (2 * pair + b + 1) * LANES)
                right[pair, :, b * LANES:(b + 1) * LANES] = build_right(q_ref[:, cols], mu_ref[0:1, cols])
        depths(jnp.int32(0), even)

        def two_steps(k, carry):
            climb(2 * k, even, 2 * k + 1, odd)
            climb(2 * k + 1, odd, jnp.minimum(2 * k + 2, pairs * STEPS - 1), even)
            return carry

        lax.fori_loop(0, pairs * STEPS // 2, two_steps, 0)

    @pl.when(lit_count == 0)
    def _():
        out_ref[...] = jnp.zeros((LEV, E), jnp.float32)

    keep.wait()


def shards(moisture, jacobian, partners, daylit, cos_zenith, albedo, absorb, rayleigh, solar):
    f32 = jnp.float32
    flat = moisture.reshape(LEV * 16, E)
    jac = jacobian.reshape(1, E)
    vmem, anywhere = pl.BlockSpec(memory_space=pltpu.VMEM), pl.BlockSpec(memory_space=pl.ANY)
    tile = (8, LANES)
    new, column_q = pl.pallas_call(
        exchange,
        in_specs=[anywhere] * 3,
        out_specs=[anywhere, vmem],
        out_shape=[jax.ShapeDtypeStruct((LEV * 16, E), f32), jax.ShapeDtypeStruct((LEV, E), f32)],
        scratch_shapes=[
            pltpu.VMEM((GROUPS, 128, E), f32),
            pltpu.VMEM((GROUPS, 8, 128, LANES), f32),
            pltpu.VMEM((GROUPS, 4, 8) + tile, f32),
            pltpu.VMEM((GROUPS, 4, 18) + tile, f32),
            pltpu.VMEM((16,) + tile, f32),
            pltpu.VMEM((5, 8) + tile, f32),
            pltpu.VMEM((2, 8) + tile, jnp.int32),
            pltpu.VMEM((2, 8) + tile, jnp.int32),
            pltpu.VMEM((1, E), f32),
            pltpu.VMEM((2, E), jnp.int32),
            pltpu.SemaphoreType.DMA((GROUPS + 2,)),
            pltpu.SemaphoreType.DMA((GROUPS,)),
            pltpu.SemaphoreType.DMA((2, GROUPS + 1)),
            pltpu.SemaphoreType.DMA((2, GROUPS + 1)),
        ],
        compiler_params=pltpu.CompilerParams(collective_id=0, has_side_effects=True, vmem_limit_bytes=60 * 2**20),
        name="exchange",
    )(flat, jac, partners)
    heating, new = pl.pallas_call(
        radiate,
        in_specs=[anywhere] + [vmem] * 6 + [anywhere],
        out_specs=[vmem, anywhere],
        out_shape=[jax.ShapeDtypeStruct((LEV, E), f32), jax.ShapeDtypeStruct((LEV * 16, E), f32)],
        scratch_shapes=[
            pltpu.VMEM((STEPS, 2 * STEP * G, 256), jnp.bfloat16),
            pltpu.VMEM((E // 256, 256, 256), jnp.bfloat16),
            pltpu.VMEM((G_BLOCKS,) + tile, f32),
            pltpu.VMEM((G_BLOCKS,) + tile, f32),
            pltpu.VMEM((2 * STEP * G, 256), f32),
            pltpu.VMEM((2 * STEP * G, 256), f32),
            pltpu.VMEM((2, G_BLOCKS) + tile, f32),
            pltpu.VMEM((2, LEV + 1) + tile, f32),
            pltpu.VMEM((LEV, E), f32),
            pltpu.VMEM((LEV * 16, E), f32),
            pltpu.SemaphoreType.DMA,
            pltpu.SemaphoreType.DMA,
            pltpu.SemaphoreType.DMA,
        ],
        compiler_params=pltpu.CompilerParams(vmem_limit_bytes=60 * 2**20),
        name="radiate",
    )(
        column_q,
        cos_zenith.reshape(1, E),
        albedo.reshape(1, E),
        daylit.reshape(1, E),
        absorb.T,
        rayleigh.reshape(1, G),
        solar.reshape(1, G),
        new,
    )
    return (new.reshape(LEV, 16, E), heating)


def solution(mesh):
    columns = P(("group", "curve"))
    placed = (
        P(None, None, ("group", "curve")),
        columns,
        P(None, ("group", "curve")),
        columns,
        columns,
        columns,
        P(),
        P(),
        P(),
    )
    return jax.shard_map(
        shards,
        mesh=mesh,
        in_specs=placed,
        out_specs=(P(None, None, ("group", "curve")), P(None, ("group", "curve"))),
        check_vma=False,
    )
```

```python
import numpy as np
import jax
import jax.numpy as jnp
from jax import lax
from jax.experimental import pallas as pl
from jax.experimental.pallas import tpu as pltpu
from jax.sharding import PartitionSpec as P

LEV, G, E = 72, 112, 1024
HALF, LANES, GROUPS = E // 2, 128, LEV // 8
ROOT5 = float(np.sqrt(5.0))
STEP_SIZE = 0.02
CROSSED = (1, 2, 13, 14)
SIDES = (4, 8, 7, 11)
G_BLOCKS = G // 8
CHAINS = G_BLOCKS // 2
STEP = 8
STEPS = LEV // STEP
RAYS = 4
AHEAD = 3
EXPONENT = -1.66 * 1.4426950408889634


def second(v):
    mean = 1.25 * ((v[0] + v[3]) - (v[1] + v[2]))
    slope = 3.75 * ((v[0] - v[3]) - ROOT5 * (v[1] - v[2]))
    inner = slope * (1.0 / ROOT5)
    return (mean + slope, mean + inner, mean - inner, mean - slope)


def take_lanes(source, index):
    return jnp.take_along_axis(source, index, axis=1)


def exchange(
    m_hbm, j_hbm, partner_hbm, new_hbm, q_ref, held, made, sides, crossed, jac, scale, inside, slot,
    j_ref, partner_ref, in_sem, out_sem, send_sem, recv_sem,
):
    me = lax.axis_index("curve")
    count = lax.axis_size("curve")
    right, left = lax.rem(me + 1, count), lax.rem(me + count - 1, count)
    blocks = E // LANES
    lane = lax.broadcasted_iota(jnp.int32, (8, LANES), 1)

    def fetch(group):
        rows = pl.ds(pl.multiple_of(group * 128, 128), 128)
        return pltpu.make_async_copy(m_hbm.at[rows], held.at[group], in_sem.at[group])

    def deliver(group):
        rows = pl.ds(pl.multiple_of(group * 128, 128), 128)
        return pltpu.make_async_copy(held.at[group], new_hbm.at[rows], out_sem.at[group])

    def send(way, group):
        return pltpu.make_async_remote_copy(
            src_ref=crossed.at[group, 2 - way],
            dst_ref=crossed.at[group, 3 * way],
            send_sem=send_sem.at[way, group],
            recv_sem=recv_sem.at[way, group],
            device_id={"curve": left if way else right},
            device_id_type=pl.DeviceIdType.MESH,
        )

    def send_jacobian(way):
        return pltpu.make_async_remote_copy(
            src_ref=jac.at[pl.ds(4 if way else 8, 4)],
            dst_ref=jac.at[pl.ds(12 if way else 0, 4)],
            send_sem=send_sem.at[way, GROUPS],
            recv_sem=recv_sem.at[way, GROUPS],
            device_id={"curve": left if way else right},
            device_id_type=pl.DeviceIdType.MESH,
        )

    barrier = pltpu.get_barrier_semaphore()
    for neighbour in (left, right):
        pl.semaphore_signal(barrier, inc=1, device_id={"curve": neighbour}, device_id_type=pl.DeviceIdType.MESH)
    small = [
        pltpu.make_async_copy(j_hbm, j_ref, in_sem.at[GROUPS]),
        pltpu.make_async_copy(partner_hbm, partner_ref, in_sem.at[GROUPS + 1]),
    ]
    for copy in small:
        copy.start()
    for group in range(AHEAD):
        fetch(group).start()
    for copy in small:
        copy.wait()
    for block in range(blocks):
        cols = pl.ds(block * LANES, LANES)
        own = jnp.broadcast_to(j_ref[:, cols], (8, LANES))
        jac[4 + block] = own
        scale[0, block] = STEP_SIZE / own
        for side in range(2):
            index = (jnp.broadcast_to(partner_ref[side:side + 1, cols], (8, LANES)) + HALF) & (E - 1)
            inside[side, block] = index & (LANES - 1)
            slot[side, block] = index >> 7

    def first_part(group):
        fetch(group).wait()
        for block in range(blocks):
            cols = pl.ds(block * LANES, LANES)
            made[group, block] = held[group, :, cols]
            node = [made[group, block, pl.ds(n, 8, stride=16), :] for n in range(16)]
            along_x = [second([node[4 * k + j] for k in range(4)]) for j in range(4)]
            along_y = [second([node[4 * i + k] for k in range(4)]) for i in range(4)]
            inverse = scale[0, block]
            corner, inner = 0.0, 0.0
            section, place = 1 + block // 4, (block % 4) * 4
            for n in range(16):
                i, j = n // 4, n % 4
                value = along_x[j][i] + along_y[i][j]
                if n in CROSSED:
                    crossed[group, section, place + CROSSED.index(n)] = value
                    continue
                if n in SIDES:
                    k = SIDES.index(n)
                    sides[group, k, block] = value
                    if block == 0 and k < 2:
                        crossed[group, 1, 16 + k] = value
                    if block == blocks - 1 and k >= 2:
                        crossed[group, 2, 16 + k - 2] = value
                    continue
                new = node[n] + inverse * value
                made[group, block, pl.ds(n, 8, stride=16), :] = new
                if i in (0, 3):
                    corner = corner + new
                else:
                    inner = inner + new
            q_ref[pl.ds(pl.multiple_of(group * 8, 8), 8), cols] = corner * (1.0 / 144.0) + inner * (25.0 / 144.0)

    first_part(0)
    pl.semaphore_wait(barrier, 2)
    for way in range(2):
        send_jacobian(way).start()
        send(way, 0).start()
    for group in range(AHEAD, AHEAD + 1):
        fetch(group).start()

    def next_group(group, carry):
        @pl.when(group + AHEAD < GROUPS)
        def _():
            fetch(group + AHEAD).start()

        first_part(group)
        for way in range(2):
            send(way, group).start()
        return carry

    lax.fori_loop(1, GROUPS, next_group, 0)

    def gather(side, block, window):
        where, which = inside[side, block], slot[side, block]
        results = None
        for k in range(blocks):
            parts = [take_lanes(source, where) for source in window(k)]
            here = which == k
            results = parts if k == 0 else [jnp.where(here, p, r) for p, r in zip(parts, results)]
        return results

    for way in range(2):
        send_jacobian(way).wait()
    for block in range(blocks):
        own = jac[4 + block]
        west = jnp.where(lane == 0, pltpu.roll(jac[3 + block], 1, 1), pltpu.roll(own, 1, 1))
        east = jnp.where(lane == LANES - 1, pltpu.roll(jac[5 + block], LANES - 1, 1), pltpu.roll(own, LANES - 1, 1))
        base = 8 * (block // 4)
        south, = gather(0, block, lambda k: [jac[base + k]])
        north, = gather(1, block, lambda k: [jac[base + k]])
        for s, other in enumerate((west, east, south, north)):
            scale[1 + s, block] = STEP_SIZE / (own + other)

    def second_part(group, carry):
        for way in range(2):
            send(way, group).wait()
        for block in range(blocks):
            cols = pl.ds(block * LANES, LANES)
            section, place = 1 + block // 4, (block % 4) * 4
            others = []
            for a in range(2):
                last = crossed[group, 0, 16 + a] if block == 0 else sides[group, 2 + a, block - 1]
                others.append(jnp.where(lane == 0, pltpu.roll(last, 1, 1), pltpu.roll(sides[group, 2 + a, block], 1, 1)))
            for a in range(2):
                following = crossed[group, 3, 16 + a] if block == blocks - 1 else sides[group, a, block + 1]
                others.append(
                    jnp.where(lane == LANES - 1, pltpu.roll(following, LANES - 1, 1), pltpu.roll(sides[group, a, block], LANES - 1, 1))
                )
            for side in range(2):
                def window(k):
                    return [crossed[group, 2 * (block // 4) + k // 4, (k % 4) * 4 + 2 * side + c] for c in (1, 0)]
                others += gather(side, block, window)
            total = 0.0
            for k, n in enumerate(SIDES + CROSSED):
                own = sides[group, k, block] if k < 4 else crossed[group, section, place + k - 4]
                new = made[group, block, pl.ds(n, 8, stride=16), :] + scale[1 + k // 2, block] * (own + others[k])
                made[group, block, pl.ds(n, 8, stride=16), :] = new
                total = total + new
            q_ref[pl.ds(pl.multiple_of(group * 8, 8), 8), cols] += total * (5.0 / 144.0)
            held[group, :, cols] = made[group, block]
        deliver(group).start()
        return carry

    lax.fori_loop(0, GROUPS, second_part, 0)

    def finish(group, carry):
        deliver(group).wait()
        return carry

    lax.fori_loop(0, GROUPS, finish, 0)


def summands(x, count):
    parts = []
    for _ in range(count):
        parts.append(x.astype(jnp.bfloat16).astype(jnp.float32))
        x = x - parts[-1]
    return parts


def short_summands(x, count):
    parts = []
    for _ in range(count):
        big = x * float(2**20 + 1)
        parts.append(big - (big - x))
        x = x - parts[-1]
    return parts


def build_left(left, absorb, ray, solar):
    high, low = summands(absorb, 2)
    rays = short_summands(ray, RAYS)
    logs = summands(jnp.log2(solar), 3)
    used = 3 * LEV + 2 * RAYS + 6
    source = jnp.concatenate(
        [high, high, low] + rays + rays + [logs[0], logs[0], logs[1], logs[1], logs[2], logs[0]]
        + [jnp.zeros((G, 256 - used), jnp.float32)],
        axis=1,
    ).astype(jnp.bfloat16)
    column = lax.broadcasted_iota(jnp.int32, (1, 256), 1)
    level_of = jnp.where(column < LEV, column, jnp.where(column < 2 * LEV, column - LEV, column - 2 * LEV))
    absorbs = column < 3 * LEV
    eights = (column >= 3 * LEV) & (column < 3 * LEV + RAYS)
    ones = (column >= 3 * LEV + RAYS) & (column < 3 * LEV + 2 * RAYS)
    for level in range(LEV):
        step, i = divmod(LEV - 1 - level, STEP)
        single = jnp.where(absorbs, (level_of == level).astype(jnp.float32), jnp.where(ones, 1.0, 0.0))
        tens, units = divmod(level + 1, 8)
        rest = jnp.where(eights, float(tens), jnp.where(ones, float(units), 1.0))
        summed = jnp.where(absorbs, (level_of <= level).astype(jnp.float32), rest)
        for kind, mask in enumerate((single, summed)):
            rows = pl.ds((kind * STEP + i) * G, G)
            left[step, rows, :] = source * jnp.broadcast_to(mask, (G, 256)).astype(jnp.bfloat16)


def build_right(q, mu):
    high, low = summands(q * q, 2)
    cos = summands(1.66 * mu, 3)
    one = jnp.ones((RAYS, LANES), jnp.float32)
    used = 3 * LEV + 2 * RAYS + 6
    rows = [high, low, high, one * 8.0, one, cos[0], cos[1], cos[0], cos[1], cos[0], cos[2]]
    return jnp.concatenate(rows + [jnp.zeros((256 - used, LANES), jnp.float32)], axis=0).astype(jnp.bfloat16)


def radiate(
    q_hbm, mu_ref, alb_ref, lit_ref, absorb_ref, ray_ref, solar_ref, new_hbm, out_ref, kept_hbm,
    left, right, half_ray, top, even, odd, climbing, net, q_ref, new_ref, q_sem, new_sem, kept_sem,
):
    fetch = pltpu.make_async_copy(q_hbm, q_ref, q_sem)
    land = pltpu.make_async_copy(new_hbm, new_ref, new_sem)
    keep = pltpu.make_async_copy(new_ref, kept_hbm, kept_sem)
    fetch.start()
    land.start()
    lit_count = jnp.sum(lit_ref[...])
    pairs = E // (2 * LANES)

    @pl.when(lit_count > 0)
    def _():
        ray = ray_ref[...].T * EXPONENT
        solar = solar_ref[...].T
        build_left(left, absorb_ref[...].T * EXPONENT, ray, solar)
        half_ray[...] = jnp.broadcast_to(ray * 0.5, (G, LANES)).reshape(G_BLOCKS, 8, LANES)
        top[...] = jnp.broadcast_to(solar, (G, LANES)).reshape(G_BLOCKS, 8, LANES)

    fetch.wait()

    def columns(pair, b):
        return pl.ds(pl.multiple_of((2 * pair + b) * LANES, LANES), LANES)

    def depths(n, buffer, piece, pieces):
        pair, step = lax.div(n, STEPS), lax.rem(n, STEPS)
        size = 2 * STEP * G // pieces
        rows = slice(piece * size, (piece + 1) * size)
        buffer[rows, :] = jnp.dot(left[step, rows, :], right[pair], preferred_element_type=jnp.float32)

    def climb(n, buffer, following, next_buffer):
        pair, step = lax.div(n, STEPS), lax.rem(n, STEPS)

        @pl.when(step == 0)
        def _():
            for b in range(2):
                climbing[b] = jnp.broadcast_to(alb_ref[0:1, columns(pair, b)][None], (G_BLOCKS, 8, LANES))

        below, totals = {}, {}
        for b in range(2):
            lanes = slice(b * LANES, (b + 1) * LANES)
            slant = jnp.broadcast_to(1.0 / (1.66 * mu_ref[0:1, columns(pair, b)]), (8, LANES))[None]
            for half in range(2):
                below[half] = climbing[b, pl.ds(half * CHAINS, CHAINS)]
            for i in range(STEP):
                if i % (STEP // 2) == 0:
                    depths(following, next_buffer, 2 * b + i // (STEP // 2), 4)
                level = LEV - 1 - step * STEP - i
                for half in range(2):
                    ray = half_ray[pl.ds(half * CHAINS, CHAINS)]
                    first = i * G + half * CHAINS * 8
                    second_kind = first + STEP * G
                    depth = buffer[first:first + CHAINS * 8, lanes].reshape(CHAINS, 8, LANES)
                    above_it = buffer[second_kind:second_kind + CHAINS * 8, lanes].reshape(CHAINS, 8, LANES)
                    totals[half] = jnp.sum(jnp.exp2(above_it * slant) * (1.0 - below[half]), axis=0)
                    diffuse = jnp.exp2(depth)
                    reflect = (ray - ray * diffuse) * (1.0 / depth)
                    below[half] = reflect + diffuse * diffuse * below[half] * (1.0 / (1.0 - reflect * below[half]))
                net[b, level + 1] = totals[0] + totals[1]
            for half in range(2):
                climbing[b, pl.ds(half * CHAINS, CHAINS)] = below[half]

        @pl.when(step == STEPS - 1)
        def _():
            for b in range(2):
                cols = columns(pair, b)
                net[b, 0] = jnp.sum(top[...] * (1.0 - climbing[b]), axis=0)
                total = jnp.sum(net[b], axis=1)
                heat = (total[:LEV] - total[1:]) * (72.0 * mu_ref[0:1, cols])
                out_ref[:, cols] = jnp.where(lit_ref[0:1, cols] == 1, heat, 0.0)

    @pl.when(lit_count > 0)
    def _():
        for pair in range(pairs):
            for b in range(2):
                cols = slice((2 * pair + b) * LANES, (2 * pair + b + 1) * LANES)
                right[pair, :, b * LANES:(b + 1) * LANES] = build_right(q_ref[:, cols], mu_ref[0:1, cols])
        depths(jnp.int32(0), even, 0, 1)

        def two_steps(k, carry):
            @pl.when(k == 2)
            def _():
                land.wait()
                keep.start()

            climb(2 * k, even, 2 * k + 1, odd)
            climb(2 * k + 1, odd, jnp.minimum(2 * k + 2, pairs * STEPS - 1), even)
            return carry

        lax.fori_loop(0, pairs * STEPS // 2, two_steps, 0)

    @pl.when(lit_count == 0)
    def _():
        land.wait()
        keep.start()
        out_ref[...] = jnp.zeros((LEV, E), jnp.float32)

    keep.wait()


def shards(moisture, jacobian, partners, daylit, cos_zenith, albedo, absorb, rayleigh, solar):
    f32 = jnp.float32
    flat = moisture.reshape(LEV * 16, E)
    jac = jacobian.reshape(1, E)
    vmem, anywhere = pl.BlockSpec(memory_space=pltpu.VMEM), pl.BlockSpec(memory_space=pl.ANY)
    tile = (8, LANES)
    new, column_q = pl.pallas_call(
        exchange,
        in_specs=[anywhere] * 3,
        out_specs=[anywhere, vmem],
        out_shape=[jax.ShapeDtypeStruct((LEV * 16, E), f32), jax.ShapeDtypeStruct((LEV, E), f32)],
        scratch_shapes=[
            pltpu.VMEM((GROUPS, 128, E), f32),
            pltpu.VMEM((GROUPS, 8, 128, LANES), f32),
            pltpu.VMEM((GROUPS, 4, 8) + tile, f32),
            pltpu.VMEM((GROUPS, 4, 18) + tile, f32),
            pltpu.VMEM((16,) + tile, f32),
            pltpu.VMEM((5, 8) + tile, f32),
            pltpu.VMEM((2, 8) + tile, jnp.int32),
            pltpu.VMEM((2, 8) + tile, jnp.int32),
            pltpu.VMEM((1, E), f32),
            pltpu.VMEM((2, E), jnp.int32),
            pltpu.SemaphoreType.DMA((GROUPS + 2,)),
            pltpu.SemaphoreType.DMA((GROUPS,)),
            pltpu.SemaphoreType.DMA((2, GROUPS + 1)),
            pltpu.SemaphoreType.DMA((2, GROUPS + 1)),
        ],
        compiler_params=pltpu.CompilerParams(collective_id=0, has_side_effects=True, vmem_limit_bytes=60 * 2**20),
        name="exchange",
    )(flat, jac, partners)
    heating, new = pl.pallas_call(
        radiate,
        in_specs=[anywhere] + [vmem] * 6 + [anywhere],
        out_specs=[vmem, anywhere],
        out_shape=[jax.ShapeDtypeStruct((LEV, E), f32), jax.ShapeDtypeStruct((LEV * 16, E), f32)],
        scratch_shapes=[
            pltpu.VMEM((STEPS, 2 * STEP * G, 256), jnp.bfloat16),
            pltpu.VMEM((E // 256, 256, 256), jnp.bfloat16),
            pltpu.VMEM((G_BLOCKS,) + tile, f32),
            pltpu.VMEM((G_BLOCKS,) + tile, f32),
            pltpu.VMEM((2 * STEP * G, 256), f32),
            pltpu.VMEM((2 * STEP * G, 256), f32),
            pltpu.VMEM((2, G_BLOCKS) + tile, f32),
            pltpu.VMEM((2, LEV + 1) + tile, f32),
            pltpu.VMEM((LEV, E), f32),
            pltpu.VMEM((LEV * 16, E), f32),
            pltpu.SemaphoreType.DMA,
            pltpu.SemaphoreType.DMA,
            pltpu.SemaphoreType.DMA,
        ],
        compiler_params=pltpu.CompilerParams(vmem_limit_bytes=60 * 2**20),
        name="radiate",
    )(
        column_q,
        cos_zenith.reshape(1, E),
        albedo.reshape(1, E),
        daylit.reshape(1, E),
        absorb.T,
        rayleigh.reshape(1, G),
        solar.reshape(1, G),
        new,
    )
    return (new.reshape(LEV, 16, E), heating)


def solution(mesh):
    columns = P(("group", "curve"))
    placed = (
        P(None, None, ("group", "curve")),
        columns,
        P(None, ("group", "curve")),
        columns,
        columns,
        columns,
        P(),
        P(),
        P(),
    )
    return jax.shard_map(
        shards,
        mesh=mesh,
        in_specs=placed,
        out_specs=(P(None, None, ("group", "curve")), P(None, ("group", "curve"))),
        check_vma=False,
    )
```

```python
import numpy as np
import jax
import jax.numpy as jnp
from jax import lax
from jax.experimental import pallas as pl
from jax.experimental.pallas import tpu as pltpu
from jax.sharding import PartitionSpec as P

LEV, G, E = 72, 112, 1024
HALF, LANES, GROUPS = E // 2, 128, LEV // 8
ROOT5 = float(np.sqrt(5.0))
STEP_SIZE = 0.02
CROSSED = (1, 2, 13, 14)
SIDES = (4, 8, 7, 11)
G_BLOCKS = G // 8
CHAINS = G_BLOCKS // 2
STEP = 8
STEPS = LEV // STEP
EIGHTS = 3 * LEV
ONES = EIGHTS + 6
LOGS = ONES + 6
AHEAD = 3
EXPONENT = -1.66 * 1.4426950408889634


def second(v):
    mean = 1.25 * ((v[0] + v[3]) - (v[1] + v[2]))
    slope = 3.75 * ((v[0] - v[3]) - ROOT5 * (v[1] - v[2]))
    inner = slope * (1.0 / ROOT5)
    return (mean + slope, mean + inner, mean - inner, mean - slope)


def take_lanes(source, index):
    return jnp.take_along_axis(source, index, axis=1)


def exchange(
    m_hbm, j_hbm, partner_hbm, new_hbm, q_ref, held, made, sides, crossed, jac, scale, inside, slot,
    j_ref, partner_ref, in_sem, out_sem, send_sem, recv_sem,
):
    me = lax.axis_index("curve")
    count = lax.axis_size("curve")
    right, left = lax.rem(me + 1, count), lax.rem(me + count - 1, count)
    blocks = E // LANES
    lane = lax.broadcasted_iota(jnp.int32, (8, LANES), 1)

    def fetch(group):
        rows = pl.ds(pl.multiple_of(group * 128, 128), 128)
        return pltpu.make_async_copy(m_hbm.at[rows], held.at[group], in_sem.at[group])

    def deliver(group):
        rows = pl.ds(pl.multiple_of(group * 128, 128), 128)
        return pltpu.make_async_copy(held.at[group], new_hbm.at[rows], out_sem.at[group])

    def send(way, group):
        return pltpu.make_async_remote_copy(
            src_ref=crossed.at[group, 2 - way],
            dst_ref=crossed.at[group, 3 * way],
            send_sem=send_sem.at[way, group],
            recv_sem=recv_sem.at[way, group],
            device_id={"curve": left if way else right},
            device_id_type=pl.DeviceIdType.MESH,
        )

    def send_jacobian(way):
        return pltpu.make_async_remote_copy(
            src_ref=jac.at[pl.ds(4 if way else 8, 4)],
            dst_ref=jac.at[pl.ds(12 if way else 0, 4)],
            send_sem=send_sem.at[way, GROUPS],
            recv_sem=recv_sem.at[way, GROUPS],
            device_id={"curve": left if way else right},
            device_id_type=pl.DeviceIdType.MESH,
        )

    barrier = pltpu.get_barrier_semaphore()
    for neighbour in (left, right):
        pl.semaphore_signal(barrier, inc=1, device_id={"curve": neighbour}, device_id_type=pl.DeviceIdType.MESH)
    small = [
        pltpu.make_async_copy(j_hbm, j_ref, in_sem.at[GROUPS]),
        pltpu.make_async_copy(partner_hbm, partner_ref, in_sem.at[GROUPS + 1]),
    ]
    for copy in small:
        copy.start()
    for group in range(AHEAD):
        fetch(group).start()
    for copy in small:
        copy.wait()
    for block in range(blocks):
        cols = pl.ds(block * LANES, LANES)
        own = jnp.broadcast_to(j_ref[:, cols], (8, LANES))
        jac[4 + block] = own
        scale[0, block] = STEP_SIZE / own
        for side in range(2):
            index = (jnp.broadcast_to(partner_ref[side:side + 1, cols], (8, LANES)) + HALF) & (E - 1)
            inside[side, block] = index & (LANES - 1)
            slot[side, block] = index >> 7

    def first_part(group):
        fetch(group).wait()
        for block in range(blocks):
            cols = pl.ds(block * LANES, LANES)
            made[group, block] = held[group, :, cols]
            node = [made[group, block, pl.ds(n, 8, stride=16), :] for n in range(16)]
            along_x = [second([node[4 * k + j] for k in range(4)]) for j in range(4)]
            along_y = [second([node[4 * i + k] for k in range(4)]) for i in range(4)]
            inverse = scale[0, block]
            corner, inner = 0.0, 0.0
            section, place = 1 + block // 4, (block % 4) * 4
            for n in range(16):
                i, j = n // 4, n % 4
                value = along_x[j][i] + along_y[i][j]
                if n in CROSSED:
                    crossed[group, section, place + CROSSED.index(n)] = value
                    continue
                if n in SIDES:
                    k = SIDES.index(n)
                    sides[group, k, block] = value
                    continue
                new = node[n] + inverse * value
                made[group, block, pl.ds(n, 8, stride=16), :] = new
                if i in (0, 3):
                    corner = corner + new
                else:
                    inner = inner + new
            q_ref[pl.ds(pl.multiple_of(group * 8, 8), 8), cols] = corner * (1.0 / 144.0) + inner * (25.0 / 144.0)
        crossed[group, 1, 16] = jnp.where(lane == 0, sides[group, 0, 0], pltpu.roll(sides[group, 1, 0], 1, 1))
        crossed[group, 2, 16] = jnp.where(
            lane == LANES - 1, sides[group, 2, blocks - 1], pltpu.roll(sides[group, 3, blocks - 1], LANES - 1, 1)
        )

    first_part(0)
    pl.semaphore_wait(barrier, 2)
    for way in range(2):
        send_jacobian(way).start()
        send(way, 0).start()
    for group in range(AHEAD, AHEAD + 1):
        fetch(group).start()

    def next_group(group, carry):
        @pl.when(group + AHEAD < GROUPS)
        def _():
            fetch(group + AHEAD).start()

        first_part(group)
        for way in range(2):
            send(way, group).start()
        return carry

    lax.fori_loop(1, GROUPS, next_group, 0)

    def gather(side, block, window):
        where, which = inside[side, block], slot[side, block]
        results = None
        for k in range(blocks):
            parts = [take_lanes(source, where) for source in window(k)]
            here = which == k
            results = parts if k == 0 else [jnp.where(here, p, r) for p, r in zip(parts, results)]
        return results

    for way in range(2):
        send_jacobian(way).wait()
    for block in range(blocks):
        own = jac[4 + block]
        west = jnp.where(lane == 0, pltpu.roll(jac[3 + block], 1, 1), pltpu.roll(own, 1, 1))
        east = jnp.where(lane == LANES - 1, pltpu.roll(jac[5 + block], LANES - 1, 1), pltpu.roll(own, LANES - 1, 1))
        base = 8 * (block // 4)
        south, = gather(0, block, lambda k: [jac[base + k]])
        north, = gather(1, block, lambda k: [jac[base + k]])
        for s, other in enumerate((west, east, south, north)):
            scale[1 + s, block] = STEP_SIZE / (own + other)

    def second_part(group, carry):
        for way in range(2):
            send(way, group).wait()
        for block in range(blocks):
            cols = pl.ds(block * LANES, LANES)
            section, place = 1 + block // 4, (block % 4) * 4
            others = []
            for a in range(2):
                if block == 0:
                    carried = pltpu.roll(crossed[group, 0, 16], 1 + a, 1)
                else:
                    carried = pltpu.roll(sides[group, 2 + a, block - 1], 1, 1)
                others.append(jnp.where(lane == 0, carried, pltpu.roll(sides[group, 2 + a, block], 1, 1)))
            for a in range(2):
                if block == blocks - 1:
                    carried = pltpu.roll(crossed[group, 3, 16], LANES - 1 - a, 1)
                else:
                    carried = pltpu.roll(sides[group, a, block + 1], LANES - 1, 1)
                others.append(jnp.where(lane == LANES - 1, carried, pltpu.roll(sides[group, a, block], LANES - 1, 1)))
            for side in range(2):
                def window(k):
                    return [crossed[group, 2 * (block // 4) + k // 4, (k % 4) * 4 + 2 * side + c] for c in (1, 0)]
                others += gather(side, block, window)
            total = 0.0
            for k, n in enumerate(SIDES + CROSSED):
                own = sides[group, k, block] if k < 4 else crossed[group, section, place + k - 4]
                new = made[group, block, pl.ds(n, 8, stride=16), :] + scale[1 + k // 2, block] * (own + others[k])
                made[group, block, pl.ds(n, 8, stride=16), :] = new
                total = total + new
            q_ref[pl.ds(pl.multiple_of(group * 8, 8), 8), cols] += total * (5.0 / 144.0)
            held[group, :, cols] = made[group, block]
        deliver(group).start()
        return carry

    lax.fori_loop(0, GROUPS, second_part, 0)

    def finish(group, carry):
        deliver(group).wait()
        return carry

    lax.fori_loop(0, GROUPS, finish, 0)


def summands(x, count):
    parts = []
    for _ in range(count):
        parts.append(x.astype(jnp.bfloat16).astype(jnp.float32))
        x = x - parts[-1]
    return parts


def short_summands(x, count):
    parts = []
    for _ in range(count):
        big = x * float(2**20 + 1)
        parts.append(big - (big - x))
        x = x - parts[-1]
    return parts


def build_left(left, absorb, ray, solar):
    high, low = summands(absorb, 2)
    rays = short_summands(ray, 4)
    rays = rays + rays[:2]
    source = jnp.concatenate(
        [high, high, low] + rays + rays + summands(jnp.log2(solar), 3) + [jnp.zeros((G, 256 - LOGS - 3), jnp.float32)], axis=1
    ).astype(jnp.bfloat16)
    column = lax.broadcasted_iota(jnp.int32, (1, 256), 1)
    level_of = jnp.where(column < LEV, column, jnp.where(column < 2 * LEV, column - LEV, column - 2 * LEV))
    absorbs = column < EIGHTS
    eights = column < ONES
    ones = column < LOGS

    def one_step(step, carry):
        for i in range(STEP):
            level = LEV - 1 - step * STEP - i
            single = jnp.where(absorbs, jnp.where(level_of == level, 1.0, 0.0), jnp.where(eights, 0.0, jnp.where(ones, 1.0, 0.0)))
            tens = (STEPS - step - (1 if i else 0)).astype(jnp.float32)
            units = float(STEP - i if i else 0)
            rest = jnp.where(eights, tens, jnp.where(ones, units, 1.0))
            summed = jnp.where(absorbs, jnp.where(level_of <= level, 1.0, 0.0), rest)
            for kind, mask in enumerate((single, summed)):
                rows = pl.ds((kind * STEP + i) * G, G)
                left[step, rows, :] = source * jnp.broadcast_to(mask, (G, 256)).astype(jnp.bfloat16)
        return carry

    lax.fori_loop(0, STEPS, one_step, 0)


def build_right(square, ray_weights, log_weight):
    high, low = summands(square, 2)
    one = jnp.ones((1, LANES), jnp.float32)
    first, second_part = (one * part for part in ray_weights)
    weights = jnp.concatenate([first] * 4 + [second_part] * 2, axis=0)
    rows = [high, low, high, weights * 8.0, weights, jnp.broadcast_to(one * log_weight, (256 - LOGS, LANES))]
    return jnp.concatenate(rows, axis=0).astype(jnp.bfloat16)


def radiate(
    q_hbm, mu_ref, alb_ref, lit_ref, absorb_ref, ray_ref, solar_ref, new_hbm, out_ref, kept_hbm,
    left, right, half_ray, top, even, odd, climbing, net, q_ref, new_ref, q_sem, new_sem, kept_sem,
):
    fetch = pltpu.make_async_copy(q_hbm, q_ref, q_sem)
    land = pltpu.make_async_copy(new_hbm, new_ref, new_sem)
    keep = pltpu.make_async_copy(new_ref, kept_hbm, kept_sem)
    fetch.start()
    land.start()
    lit_count = jnp.sum(lit_ref[...])
    pairs = E // (2 * LANES)

    @pl.when(lit_count > 0)
    def _():
        ray = ray_ref[...].T * EXPONENT
        solar = solar_ref[...].T
        build_left(left, absorb_ref[...].T * EXPONENT, ray, solar)
        half_ray[...] = jnp.broadcast_to(ray * 0.5, (G, LANES)).reshape(G_BLOCKS, 8, LANES)
        top[...] = jnp.broadcast_to(solar, (G, LANES)).reshape(G_BLOCKS, 8, LANES)

    fetch.wait()

    def columns(pair, b):
        return pl.ds(pl.multiple_of((2 * pair + b) * LANES, LANES), LANES)

    def depths(n, buffer, piece):
        pair, step = lax.div(n, STEPS), lax.rem(n, STEPS)
        size = 2 * STEP * G // 4
        rows = slice(piece * size, (piece + 1) * size)
        buffer[rows, :] = jnp.dot(left[step, rows, :], right[piece // 2, pair], preferred_element_type=jnp.float32)

    def climb(n, buffer, following, next_buffer):
        pair, step = lax.div(n, STEPS), lax.rem(n, STEPS)

        @pl.when(step == 0)
        def _():
            for b in range(2):
                climbing[b] = jnp.broadcast_to(alb_ref[0:1, columns(pair, b)][None], (G_BLOCKS, 8, LANES))

        below, totals = {}, {}
        for b in range(2):
            lanes = slice(b * LANES, (b + 1) * LANES)
            for half in range(2):
                below[half] = climbing[b, pl.ds(half * CHAINS, CHAINS)]
            for i in range(STEP):
                if i % (STEP // 2) == 0:
                    depths(following, next_buffer, 2 * b + i // (STEP // 2))
                level = LEV - 1 - step * STEP - i
                for half in range(2):
                    ray = half_ray[pl.ds(half * CHAINS, CHAINS)]
                    first = i * G + half * CHAINS * 8
                    second_kind = first + STEP * G
                    depth = buffer[first:first + CHAINS * 8, lanes].reshape(CHAINS, 8, LANES)
                    above_it = buffer[second_kind:second_kind + CHAINS * 8, lanes].reshape(CHAINS, 8, LANES)
                    totals[half] = jnp.sum(jnp.exp2(above_it) * (1.0 - below[half]), axis=0)
                    diffuse = jnp.exp2(depth)
                    reflect = (ray - ray * diffuse) * (1.0 / depth)
                    below[half] = reflect + diffuse * diffuse * below[half] * (1.0 / (1.0 - reflect * below[half]))
                net[b, level + 1] = totals[0] + totals[1]
            for half in range(2):
                climbing[b, pl.ds(half * CHAINS, CHAINS)] = below[half]

        @pl.when(step == STEPS - 1)
        def _():
            for b in range(2):
                cols = columns(pair, b)
                net[b, 0] = jnp.sum(top[...] * (1.0 - climbing[b]), axis=0)
                total = jnp.sum(net[b], axis=1)
                heat = (total[:LEV] - total[1:]) * (72.0 * mu_ref[0:1, cols])
                out_ref[:, cols] = jnp.where(lit_ref[0:1, cols] == 1, heat, 0.0)

    @pl.when(lit_count > 0)
    def _():
        for pair in range(pairs):
            for b in range(2):
                cols = slice((2 * pair + b) * LANES, (2 * pair + b + 1) * LANES)
                square = q_ref[:, cols]
                square = square * square
                slant = 1.0 / (1.66 * mu_ref[0:1, cols])
                lanes = slice(b * LANES, (b + 1) * LANES)
                right[0, pair, :, lanes] = build_right(square, (1.0, 0.0), 0.0)
                right[1, pair, :, lanes] = build_right(square * slant, summands(slant, 2), 1.0)
        for piece in range(4):
            depths(jnp.int32(0), even, piece)

        def two_steps(k, carry):
            @pl.when(k == 2)
            def _():
                land.wait()
                keep.start()

            climb(2 * k, even, 2 * k + 1, odd)
            climb(2 * k + 1, odd, jnp.minimum(2 * k + 2, pairs * STEPS - 1), even)
            return carry

        lax.fori_loop(0, pairs * STEPS // 2, two_steps, 0)

    @pl.when(lit_count == 0)
    def _():
        land.wait()
        keep.start()
        out_ref[...] = jnp.zeros((LEV, E), jnp.float32)

    keep.wait()


def shards(moisture, jacobian, partners, daylit, cos_zenith, albedo, absorb, rayleigh, solar):
    f32 = jnp.float32
    flat = moisture.reshape(LEV * 16, E)
    jac = jacobian.reshape(1, E)
    vmem, anywhere = pl.BlockSpec(memory_space=pltpu.VMEM), pl.BlockSpec(memory_space=pl.ANY)
    tile = (8, LANES)
    new, column_q = pl.pallas_call(
        exchange,
        in_specs=[anywhere] * 3,
        out_specs=[anywhere, vmem],
        out_shape=[jax.ShapeDtypeStruct((LEV * 16, E), f32), jax.ShapeDtypeStruct((LEV, E), f32)],
        scratch_shapes=[
            pltpu.VMEM((GROUPS, 128, E), f32),
            pltpu.VMEM((GROUPS, 8, 128, LANES), f32),
            pltpu.VMEM((GROUPS, 4, 8) + tile, f32),
            pltpu.VMEM((GROUPS, 4, 17) + tile, f32),
            pltpu.VMEM((16,) + tile, f32),
            pltpu.VMEM((5, 8) + tile, f32),
            pltpu.VMEM((2, 8) + tile, jnp.int32),
            pltpu.VMEM((2, 8) + tile, jnp.int32),
            pltpu.VMEM((1, E), f32),
            pltpu.VMEM((2, E), jnp.int32),
            pltpu.SemaphoreType.DMA((GROUPS + 2,)),
            pltpu.SemaphoreType.DMA((GROUPS,)),
            pltpu.SemaphoreType.DMA((2, GROUPS + 1)),
            pltpu.SemaphoreType.DMA((2, GROUPS + 1)),
        ],
        compiler_params=pltpu.CompilerParams(collective_id=0, has_side_effects=True, vmem_limit_bytes=60 * 2**20),
        name="exchange",
    )(flat, jac, partners)
    heating, new = pl.pallas_call(
        radiate,
        in_specs=[anywhere] + [vmem] * 6 + [anywhere],
        out_specs=[vmem, anywhere],
        out_shape=[jax.ShapeDtypeStruct((LEV, E), f32), jax.ShapeDtypeStruct((LEV * 16, E), f32)],
        scratch_shapes=[
            pltpu.VMEM((STEPS, 2 * STEP * G, 256), jnp.bfloat16),
            pltpu.VMEM((2, E // 256, 256, 256), jnp.bfloat16),
            pltpu.VMEM((G_BLOCKS,) + tile, f32),
            pltpu.VMEM((G_BLOCKS,) + tile, f32),
            pltpu.VMEM((2 * STEP * G, 256), f32),
            pltpu.VMEM((2 * STEP * G, 256), f32),
            pltpu.VMEM((2, G_BLOCKS) + tile, f32),
            pltpu.VMEM((2, LEV + 1) + tile, f32),
            pltpu.VMEM((LEV, E), f32),
            pltpu.VMEM((LEV * 16, E), f32),
            pltpu.SemaphoreType.DMA,
            pltpu.SemaphoreType.DMA,
            pltpu.SemaphoreType.DMA,
        ],
        compiler_params=pltpu.CompilerParams(vmem_limit_bytes=60 * 2**20),
        name="radiate",
    )(
        column_q,
        cos_zenith.reshape(1, E),
        albedo.reshape(1, E),
        daylit.reshape(1, E),
        absorb.T,
        rayleigh.reshape(1, G),
        solar.reshape(1, G),
        new,
    )
    return (new.reshape(LEV, 16, E), heating)


def solution(mesh):
    columns = P(("group", "curve"))
    placed = (
        P(None, None, ("group", "curve")),
        columns,
        P(None, ("group", "curve")),
        columns,
        columns,
        columns,
        P(),
        P(),
        P(),
    )
    return jax.shard_map(
        shards,
        mesh=mesh,
        in_specs=placed,
        out_specs=(P(None, None, ("group", "curve")), P(None, ("group", "curve"))),
        check_vma=False,
    )
```

```python
import numpy as np
import jax
import jax.numpy as jnp
from jax import lax
from jax.experimental import pallas as pl
from jax.experimental.pallas import tpu as pltpu
from jax.sharding import PartitionSpec as P

LEV, G, E = 72, 112, 1024
HALF, LANES, GROUPS = E // 2, 128, LEV // 8
ROOT5 = float(np.sqrt(5.0))
STEP_SIZE = 0.02
CROSSED = (1, 2, 13, 14)
SIDES = (4, 8, 7, 11)
G_BLOCKS = G // 8
CHAINS = G_BLOCKS // 2
STEP = 18
STEPS = LEV // STEP
EIGHTS = 3 * LEV
ONES = EIGHTS + 6
LOGS = ONES + 6
AHEAD = 3
EXPONENT = -1.66 * 1.4426950408889634


def second(v):
    mean = 1.25 * ((v[0] + v[3]) - (v[1] + v[2]))
    slope = 3.75 * ((v[0] - v[3]) - ROOT5 * (v[1] - v[2]))
    inner = slope * (1.0 / ROOT5)
    return (mean + slope, mean + inner, mean - inner, mean - slope)


def take_lanes(source, index):
    return jnp.take_along_axis(source, index, axis=1)


def exchange(
    m_hbm, j_hbm, partner_hbm, new_hbm, q_ref, held, made, sides, crossed, jac, scale, inside, slot,
    j_ref, partner_ref, in_sem, out_sem, send_sem, recv_sem,
):
    me = lax.axis_index("curve")
    count = lax.axis_size("curve")
    right, left = lax.rem(me + 1, count), lax.rem(me + count - 1, count)
    blocks = E // LANES
    lane = lax.broadcasted_iota(jnp.int32, (8, LANES), 1)

    def fetch(group):
        rows = pl.ds(pl.multiple_of(group * 128, 128), 128)
        return pltpu.make_async_copy(m_hbm.at[rows], held.at[group], in_sem.at[group])

    def deliver(group):
        rows = pl.ds(pl.multiple_of(group * 128, 128), 128)
        return pltpu.make_async_copy(held.at[group], new_hbm.at[rows], out_sem.at[group])

    def send(way, group):
        return pltpu.make_async_remote_copy(
            src_ref=crossed.at[group, 2 - way],
            dst_ref=crossed.at[group, 3 * way],
            send_sem=send_sem.at[way, group],
            recv_sem=recv_sem.at[way, group],
            device_id={"curve": left if way else right},
            device_id_type=pl.DeviceIdType.MESH,
        )

    def send_jacobian(way):
        return pltpu.make_async_remote_copy(
            src_ref=jac.at[pl.ds(4 if way else 8, 4)],
            dst_ref=jac.at[pl.ds(12 if way else 0, 4)],
            send_sem=send_sem.at[way, GROUPS],
            recv_sem=recv_sem.at[way, GROUPS],
            device_id={"curve": left if way else right},
            device_id_type=pl.DeviceIdType.MESH,
        )

    barrier = pltpu.get_barrier_semaphore()
    for neighbour in (left, right):
        pl.semaphore_signal(barrier, inc=1, device_id={"curve": neighbour}, device_id_type=pl.DeviceIdType.MESH)
    small = [
        pltpu.make_async_copy(j_hbm, j_ref, in_sem.at[GROUPS]),
        pltpu.make_async_copy(partner_hbm, partner_ref, in_sem.at[GROUPS + 1]),
    ]
    for copy in small:
        copy.start()
    for group in range(AHEAD):
        fetch(group).start()
    for copy in small:
        copy.wait()
    for block in range(blocks):
        cols = pl.ds(block * LANES, LANES)
        own = jnp.broadcast_to(j_ref[:, cols], (8, LANES))
        jac[4 + block] = own
        scale[0, block] = STEP_SIZE / own
        for side in range(2):
            index = (jnp.broadcast_to(partner_ref[side:side + 1, cols], (8, LANES)) + HALF) & (E - 1)
            inside[side, block] = index & (LANES - 1)
            slot[side, block] = index >> 7

    def first_part(group):
        fetch(group).wait()
        for block in range(blocks):
            cols = pl.ds(block * LANES, LANES)
            made[group, block] = held[group, :, cols]
            node = [made[group, block, pl.ds(n, 8, stride=16), :] for n in range(16)]
            along_x = [second([node[4 * k + j] for k in range(4)]) for j in range(4)]
            along_y = [second([node[4 * i + k] for k in range(4)]) for i in range(4)]
            inverse = scale[0, block]
            corner, inner = 0.0, 0.0
            section, place = 1 + block // 4, (block % 4) * 4
            for n in range(16):
                i, j = n // 4, n % 4
                value = along_x[j][i] + along_y[i][j]
                if n in CROSSED:
                    crossed[group, section, place + CROSSED.index(n)] = value
                    continue
                if n in SIDES:
                    k = SIDES.index(n)
                    sides[group, k, block] = value
                    continue
                new = node[n] + inverse * value
                made[group, block, pl.ds(n, 8, stride=16), :] = new
                if i in (0, 3):
                    corner = corner + new
                else:
                    inner = inner + new
            q_ref[pl.ds(pl.multiple_of(group * 8, 8), 8), cols] = corner * (1.0 / 144.0) + inner * (25.0 / 144.0)
        crossed[group, 1, 16] = jnp.where(lane == 0, sides[group, 0, 0], pltpu.roll(sides[group, 1, 0], 1, 1))
        crossed[group, 2, 16] = jnp.where(
            lane == LANES - 1, sides[group, 2, blocks - 1], pltpu.roll(sides[group, 3, blocks - 1], LANES - 1, 1)
        )

    first_part(0)
    pl.semaphore_wait(barrier, 2)
    for way in range(2):
        send_jacobian(way).start()
        send(way, 0).start()
    for group in range(AHEAD, AHEAD + 1):
        fetch(group).start()

    def next_group(group, carry):
        @pl.when(group + AHEAD < GROUPS)
        def _():
            fetch(group + AHEAD).start()

        first_part(group)
        for way in range(2):
            send(way, group).start()
        return carry

    lax.fori_loop(1, GROUPS, next_group, 0)

    def gather(side, block, window):
        where, which = inside[side, block], slot[side, block]
        results = None
        for k in range(blocks):
            parts = [take_lanes(source, where) for source in window(k)]
            here = which == k
            results = parts if k == 0 else [jnp.where(here, p, r) for p, r in zip(parts, results)]
        return results

    for way in range(2):
        send_jacobian(way).wait()
    for block in range(blocks):
        own = jac[4 + block]
        west = jnp.where(lane == 0, pltpu.roll(jac[3 + block], 1, 1), pltpu.roll(own, 1, 1))
        east = jnp.where(lane == LANES - 1, pltpu.roll(jac[5 + block], LANES - 1, 1), pltpu.roll(own, LANES - 1, 1))
        base = 8 * (block // 4)
        south, = gather(0, block, lambda k: [jac[base + k]])
        north, = gather(1, block, lambda k: [jac[base + k]])
        for s, other in enumerate((west, east, south, north)):
            scale[1 + s, block] = STEP_SIZE / (own + other)

    def second_part(group, carry):
        for way in range(2):
            send(way, group).wait()
        eastern = [[pltpu.roll(crossed[group, 0, 16], 1 + a, 1) for a in range(2)]]
        for block in range(blocks):
            cols = pl.ds(block * LANES, LANES)
            section, place = 1 + block // 4, (block % 4) * 4
            eastern.append([pltpu.roll(sides[group, 2 + a, block], 1, 1) for a in range(2)])
            if block == 0:
                western = [pltpu.roll(sides[group, a, 0], LANES - 1, 1) for a in range(2)]
            if block == blocks - 1:
                later = [pltpu.roll(crossed[group, 3, 16], LANES - 1 - a, 1) for a in range(2)]
            else:
                later = [pltpu.roll(sides[group, a, block + 1], LANES - 1, 1) for a in range(2)]
            others = [jnp.where(lane == 0, eastern[block][a], eastern[block + 1][a]) for a in range(2)]
            others += [jnp.where(lane == LANES - 1, later[a], western[a]) for a in range(2)]
            western = later
            for side in range(2):
                def window(k):
                    return [crossed[group, 2 * (block // 4) + k // 4, (k % 4) * 4 + 2 * side + c] for c in (1, 0)]
                others += gather(side, block, window)
            total = 0.0
            for k, n in enumerate(SIDES + CROSSED):
                own = sides[group, k, block] if k < 4 else crossed[group, section, place + k - 4]
                new = made[group, block, pl.ds(n, 8, stride=16), :] + scale[1 + k // 2, block] * (own + others[k])
                made[group, block, pl.ds(n, 8, stride=16), :] = new
                total = total + new
            q_ref[pl.ds(pl.multiple_of(group * 8, 8), 8), cols] += total * (5.0 / 144.0)
            held[group, :, cols] = made[group, block]
        deliver(group).start()
        return carry

    lax.fori_loop(0, GROUPS, second_part, 0)

    def finish(group, carry):
        deliver(group).wait()
        return carry

    lax.fori_loop(0, GROUPS, finish, 0)


def summands(x, count):
    parts = []
    for _ in range(count):
        parts.append(x.astype(jnp.bfloat16).astype(jnp.float32))
        x = x - parts[-1]
    return parts


def short_summands(x, count):
    parts = []
    for _ in range(count):
        big = x * float(2**20 + 1)
        parts.append(big - (big - x))
        x = x - parts[-1]
    return parts


def build_left(left, absorb, ray, solar):
    high, low = summands(absorb, 2)
    rays = short_summands(ray, 4)
    rays = rays + rays[:2]
    source = jnp.concatenate(
        [high, high, low] + rays + rays + summands(jnp.log2(solar), 3) + [jnp.zeros((G, 256 - LOGS - 3), jnp.float32)], axis=1
    ).astype(jnp.bfloat16)
    column = lax.broadcasted_iota(jnp.int32, (1, 256), 1)
    level_of = jnp.where(column < LEV, column, jnp.where(column < 2 * LEV, column - LEV, column - 2 * LEV))
    absorbs = column < EIGHTS
    eights = column < ONES
    ones = column < LOGS

    def one_step(step, carry):
        for i in range(STEP):
            level = LEV - 1 - step * STEP - i
            single = jnp.where(absorbs, jnp.where(level_of == level, 1.0, 0.0), jnp.where(eights, 0.0, jnp.where(ones, 1.0, 0.0)))
            tens = lax.div(level + 1, 8).astype(jnp.float32)
            units = lax.rem(level + 1, 8).astype(jnp.float32)
            rest = jnp.where(eights, tens, jnp.where(ones, units, 1.0))
            summed = jnp.where(absorbs, jnp.where(level_of <= level, 1.0, 0.0), rest)
            for kind, mask in enumerate((single, summed)):
                rows = pl.ds((kind * STEP + i) * G, G)
                left[step, rows, :] = source * jnp.broadcast_to(mask, (G, 256)).astype(jnp.bfloat16)
        return carry

    lax.fori_loop(0, STEPS, one_step, 0)


def build_right(square, ray_weights, log_weight):
    high, low = summands(square, 2)
    one = jnp.ones((1, LANES), jnp.float32)
    first, second_part = (one * part for part in ray_weights)
    weights = jnp.concatenate([first] * 4 + [second_part] * 2, axis=0)
    rows = [high, low, high, weights * 8.0, weights, jnp.broadcast_to(one * log_weight, (256 - LOGS, LANES))]
    return jnp.concatenate(rows, axis=0).astype(jnp.bfloat16)


def sublane_sums(arrays):
    row = lax.broadcasted_iota(jnp.int32, (8, LANES), 0)
    for size in (4, 2, 1):
        lower = (row & size) == 0
        joined = []
        for x, y in zip(arrays[:size], arrays[size:]):
            swapped = jnp.where(lower, y, x)
            if size == 4:
                moved = pltpu.roll(swapped, 4, 0)
            else:
                moved = jnp.where(lower, pltpu.roll(swapped, 8 - size, 0), pltpu.roll(swapped, size, 0))
            joined.append(jnp.where(lower, x, y) + moved)
        arrays = joined
    return arrays[0]


def radiate(
    q_hbm, mu_ref, alb_ref, lit_ref, absorb_ref, ray_ref, solar_ref, new_hbm, out_ref, kept_hbm,
    left, right, half_ray, top, even, odd, climbing, net, q_ref, new_ref, q_sem, new_sem, kept_sem,
):
    fetch = pltpu.make_async_copy(q_hbm, q_ref, q_sem)
    land = pltpu.make_async_copy(new_hbm, new_ref, new_sem)
    keep = pltpu.make_async_copy(new_ref, kept_hbm, kept_sem)
    fetch.start()
    land.start()
    lit_count = jnp.sum(lit_ref[...])
    pairs = E // (2 * LANES)

    @pl.when(lit_count > 0)
    def _():
        ray = ray_ref[...].T * EXPONENT
        solar = solar_ref[...].T
        build_left(left, absorb_ref[...].T * EXPONENT, ray, solar)
        half_ray[...] = jnp.broadcast_to(ray * 0.5, (G, LANES)).reshape(G_BLOCKS, 8, LANES)
        top[...] = jnp.broadcast_to(solar, (G, LANES)).reshape(G_BLOCKS, 8, LANES)

    fetch.wait()

    def columns(pair, b):
        return pl.ds(pl.multiple_of((2 * pair + b) * LANES, LANES), LANES)

    def depths(n, buffer, piece):
        pair, step = lax.div(n, STEPS), lax.rem(n, STEPS)
        size = 2 * STEP * G // 4
        rows = slice(piece * size, (piece + 1) * size)
        buffer[rows, :] = jnp.dot(left[step, rows, :], right[piece // 2, pair], preferred_element_type=jnp.float32)

    def climb(n, buffer, following, next_buffer):
        pair, step = lax.div(n, STEPS), lax.rem(n, STEPS)

        @pl.when(step == 0)
        def _():
            for b in range(2):
                climbing[b] = jnp.broadcast_to(alb_ref[0:1, columns(pair, b)][None], (G_BLOCKS, 8, LANES))

        below, totals = {}, {}
        for b in range(2):
            lanes = slice(b * LANES, (b + 1) * LANES)
            for half in range(2):
                below[half] = climbing[b, pl.ds(half * CHAINS, CHAINS)]
            for i in range(STEP):
                if i % (STEP // 2) == 0:
                    depths(following, next_buffer, 2 * b + i // (STEP // 2))
                level = LEV - 1 - step * STEP - i
                for half in range(2):
                    ray = half_ray[pl.ds(half * CHAINS, CHAINS)]
                    first = i * G + half * CHAINS * 8
                    second_kind = first + STEP * G
                    depth = buffer[first:first + CHAINS * 8, lanes].reshape(CHAINS, 8, LANES)
                    above_it = buffer[second_kind:second_kind + CHAINS * 8, lanes].reshape(CHAINS, 8, LANES)
                    totals[half] = jnp.sum(jnp.exp2(above_it) * (1.0 - below[half]), axis=0)
                    diffuse = jnp.exp2(depth)
                    reflect = (ray - ray * diffuse) * (1.0 / depth)
                    below[half] = reflect + diffuse * diffuse * below[half] * (1.0 / (1.0 - reflect * below[half]))
                net[b, level + 1] = totals[0] + totals[1]
            for half in range(2):
                climbing[b, pl.ds(half * CHAINS, CHAINS)] = below[half]

        @pl.when(step == STEPS - 1)
        def _():
            for b in range(2):
                cols = columns(pair, b)
                net[b, 0] = jnp.sum(top[...] * (1.0 - climbing[b]), axis=0)
                total = jnp.concatenate(
                    [sublane_sums([net[b, 8 * k + i] for i in range(8)]) for k in range(LEV // 8)]
                    + [jnp.sum(net[b, LEV], axis=0, keepdims=True)],
                    axis=0,
                )
                heat = (total[:LEV] - total[1:]) * (72.0 * mu_ref[0:1, cols])
                out_ref[:, cols] = jnp.where(lit_ref[0:1, cols] == 1, heat, 0.0)

    @pl.when(lit_count > 0)
    def _():
        for pair in range(pairs):
            for b in range(2):
                cols = slice((2 * pair + b) * LANES, (2 * pair + b + 1) * LANES)
                square = q_ref[:, cols]
                square = square * square
                slant = 1.0 / (1.66 * mu_ref[0:1, cols])
                lanes = slice(b * LANES, (b + 1) * LANES)
                right[0, pair, :, lanes] = build_right(square, (1.0, 0.0), 0.0)
                right[1, pair, :, lanes] = build_right(square * slant, summands(slant, 2), 1.0)
        for piece in range(4):
            depths(jnp.int32(0), even, piece)

        def two_steps(k, carry):
            @pl.when(k == 2)
            def _():
                land.wait()
                keep.start()

            climb(2 * k, even, 2 * k + 1, odd)
            climb(2 * k + 1, odd, jnp.minimum(2 * k + 2, pairs * STEPS - 1), even)
            return carry

        lax.fori_loop(0, pairs * STEPS // 2, two_steps, 0)

    @pl.when(lit_count == 0)
    def _():
        land.wait()
        keep.start()
        out_ref[...] = jnp.zeros((LEV, E), jnp.float32)

    keep.wait()


def shards(moisture, jacobian, partners, daylit, cos_zenith, albedo, absorb, rayleigh, solar):
    f32 = jnp.float32
    flat = moisture.reshape(LEV * 16, E)
    jac = jacobian.reshape(1, E)
    vmem, anywhere = pl.BlockSpec(memory_space=pltpu.VMEM), pl.BlockSpec(memory_space=pl.ANY)
    tile = (8, LANES)
    new, column_q = pl.pallas_call(
        exchange,
        in_specs=[anywhere] * 3,
        out_specs=[anywhere, vmem],
        out_shape=[jax.ShapeDtypeStruct((LEV * 16, E), f32), jax.ShapeDtypeStruct((LEV, E), f32)],
        scratch_shapes=[
            pltpu.VMEM((GROUPS, 128, E), f32),
            pltpu.VMEM((GROUPS, 8, 128, LANES), f32),
            pltpu.VMEM((GROUPS, 4, 8) + tile, f32),
            pltpu.VMEM((GROUPS, 4, 17) + tile, f32),
            pltpu.VMEM((16,) + tile, f32),
            pltpu.VMEM((5, 8) + tile, f32),
            pltpu.VMEM((2, 8) + tile, jnp.int32),
            pltpu.VMEM((2, 8) + tile, jnp.int32),
            pltpu.VMEM((1, E), f32),
            pltpu.VMEM((2, E), jnp.int32),
            pltpu.SemaphoreType.DMA((GROUPS + 2,)),
            pltpu.SemaphoreType.DMA((GROUPS,)),
            pltpu.SemaphoreType.DMA((2, GROUPS + 1)),
            pltpu.SemaphoreType.DMA((2, GROUPS + 1)),
        ],
        compiler_params=pltpu.CompilerParams(collective_id=0, has_side_effects=True, vmem_limit_bytes=60 * 2**20),
        name="exchange",
    )(flat, jac, partners)
    heating, new = pl.pallas_call(
        radiate,
        in_specs=[anywhere] + [vmem] * 6 + [anywhere],
        out_specs=[vmem, anywhere],
        out_shape=[jax.ShapeDtypeStruct((LEV, E), f32), jax.ShapeDtypeStruct((LEV * 16, E), f32)],
        scratch_shapes=[
            pltpu.VMEM((STEPS, 2 * STEP * G, 256), jnp.bfloat16),
            pltpu.VMEM((2, E // 256, 256, 256), jnp.bfloat16),
            pltpu.VMEM((G_BLOCKS,) + tile, f32),
            pltpu.VMEM((G_BLOCKS,) + tile, f32),
            pltpu.VMEM((2 * STEP * G, 256), f32),
            pltpu.VMEM((2 * STEP * G, 256), f32),
            pltpu.VMEM((2, G_BLOCKS) + tile, f32),
            pltpu.VMEM((2, LEV + 1) + tile, f32),
            pltpu.VMEM((LEV, E), f32),
            pltpu.VMEM((LEV * 16, E), f32),
            pltpu.SemaphoreType.DMA,
            pltpu.SemaphoreType.DMA,
            pltpu.SemaphoreType.DMA,
        ],
        compiler_params=pltpu.CompilerParams(vmem_limit_bytes=60 * 2**20),
        name="radiate",
    )(
        column_q,
        cos_zenith.reshape(1, E),
        albedo.reshape(1, E),
        daylit.reshape(1, E),
        absorb.T,
        rayleigh.reshape(1, G),
        solar.reshape(1, G),
        new,
    )
    return (new.reshape(LEV, 16, E), heating)


def solution(mesh):
    columns = P(("group", "curve"))
    placed = (
        P(None, None, ("group", "curve")),
        columns,
        P(None, ("group", "curve")),
        columns,
        columns,
        columns,
        P(),
        P(),
        P(),
    )
    return jax.shard_map(
        shards,
        mesh=mesh,
        in_specs=placed,
        out_specs=(P(None, None, ("group", "curve")), P(None, ("group", "curve"))),
        check_vma=False,
    )
```

```python
import numpy as np
import jax
import jax.numpy as jnp
from jax import lax
from jax.experimental import pallas as pl
from jax.experimental.pallas import tpu as pltpu
from jax.sharding import PartitionSpec as P

LEV, G, E = 72, 112, 1024
HALF, LANES, GROUPS = E // 2, 128, LEV // 8
ROOT5 = float(np.sqrt(5.0))
STEP_SIZE = 0.02
CROSSED = (1, 2, 13, 14)
SIDES = (4, 8, 7, 11)
G_BLOCKS = G // 8
CHAINS = G_BLOCKS // 2
STEP = 18
STEPS = LEV // STEP
EIGHTS = 3 * LEV
ONES = EIGHTS + 6
LOGS = ONES + 6
AHEAD = 3
EXPONENT = -1.66 * 1.4426950408889634


def second(v):
    mean = 1.25 * ((v[0] + v[3]) - (v[1] + v[2]))
    slope = 3.75 * ((v[0] - v[3]) - ROOT5 * (v[1] - v[2]))
    inner = slope * (1.0 / ROOT5)
    return (mean + slope, mean + inner, mean - inner, mean - slope)


def take_lanes(source, index):
    return jnp.take_along_axis(source, index, axis=1)


def exchange(
    m_hbm, j_hbm, partner_hbm, new_hbm, q_ref, held, made, sides, crossed, jac, scale, inside, slot,
    j_ref, partner_ref, in_sem, out_sem, send_sem, recv_sem,
):
    me = lax.axis_index("curve")
    count = lax.axis_size("curve")
    right, left = lax.rem(me + 1, count), lax.rem(me + count - 1, count)
    blocks = E // LANES
    lane = lax.broadcasted_iota(jnp.int32, (8, LANES), 1)

    def fetch(group):
        rows = pl.ds(pl.multiple_of(group * 128, 128), 128)
        return pltpu.make_async_copy(m_hbm.at[rows], held.at[group], in_sem.at[group])

    def deliver(group):
        rows = pl.ds(pl.multiple_of(group * 128, 128), 128)
        return pltpu.make_async_copy(held.at[group], new_hbm.at[rows], out_sem.at[group])

    def send(way, group):
        return pltpu.make_async_remote_copy(
            src_ref=crossed.at[group, 2 - way],
            dst_ref=crossed.at[group, 3 * way],
            send_sem=send_sem.at[way, group],
            recv_sem=recv_sem.at[way, group],
            device_id={"curve": left if way else right},
            device_id_type=pl.DeviceIdType.MESH,
        )

    def send_jacobian(way):
        return pltpu.make_async_remote_copy(
            src_ref=jac.at[pl.ds(4 if way else 8, 4)],
            dst_ref=jac.at[pl.ds(12 if way else 0, 4)],
            send_sem=send_sem.at[way, GROUPS],
            recv_sem=recv_sem.at[way, GROUPS],
            device_id={"curve": left if way else right},
            device_id_type=pl.DeviceIdType.MESH,
        )

    barrier = pltpu.get_barrier_semaphore()
    for neighbour in (left, right):
        pl.semaphore_signal(barrier, inc=1, device_id={"curve": neighbour}, device_id_type=pl.DeviceIdType.MESH)
    small = [
        pltpu.make_async_copy(j_hbm, j_ref, in_sem.at[GROUPS]),
        pltpu.make_async_copy(partner_hbm, partner_ref, in_sem.at[GROUPS + 1]),
    ]
    for copy in small:
        copy.start()
    fetch(0).start()
    for copy in small:
        copy.wait()
    for group in range(1, AHEAD):
        fetch(group).start()
    for block in range(blocks):
        cols = pl.ds(block * LANES, LANES)
        own = jnp.broadcast_to(j_ref[:, cols], (8, LANES))
        jac[4 + block] = own
        scale[0, block] = STEP_SIZE / own
        for side in range(2):
            index = (jnp.broadcast_to(partner_ref[side:side + 1, cols], (8, LANES)) + HALF) & (E - 1)
            inside[side, block] = index & (LANES - 1)
            slot[side, block] = index >> 7

    def first_part(group):
        fetch(group).wait()
        for block in range(blocks):
            cols = pl.ds(block * LANES, LANES)
            made[group, block] = held[group, :, cols]
            node = [made[group, block, pl.ds(n, 8, stride=16), :] for n in range(16)]
            along_x = [second([node[4 * k + j] for k in range(4)]) for j in range(4)]
            along_y = [second([node[4 * i + k] for k in range(4)]) for i in range(4)]
            inverse = scale[0, block]
            corner, inner = 0.0, 0.0
            section, place = 1 + block // 4, (block % 4) * 4
            for n in range(16):
                i, j = n // 4, n % 4
                value = along_x[j][i] + along_y[i][j]
                if n in CROSSED:
                    crossed[group, section, place + CROSSED.index(n)] = value
                    continue
                if n in SIDES:
                    k = SIDES.index(n)
                    sides[group, k, block] = value
                    continue
                new = node[n] + inverse * value
                made[group, block, pl.ds(n, 8, stride=16), :] = new
                if i in (0, 3):
                    corner = corner + new
                else:
                    inner = inner + new
            q_ref[pl.ds(pl.multiple_of(group * 8, 8), 8), cols] = corner * (1.0 / 144.0) + inner * (25.0 / 144.0)
        crossed[group, 1, 16] = jnp.where(lane == 0, sides[group, 0, 0], pltpu.roll(sides[group, 1, 0], 1, 1))
        crossed[group, 2, 16] = jnp.where(
            lane == LANES - 1, sides[group, 2, blocks - 1], pltpu.roll(sides[group, 3, blocks - 1], LANES - 1, 1)
        )

    first_part(0)
    pl.semaphore_wait(barrier, 2)
    for way in range(2):
        send(way, 0).start()
        send_jacobian(way).start()
    for group in range(AHEAD, AHEAD + 1):
        fetch(group).start()

    def next_group(group, carry):
        @pl.when(group + AHEAD < GROUPS)
        def _():
            fetch(group + AHEAD).start()

        first_part(group)
        for way in range(2):
            send(way, group).start()
        return carry

    lax.fori_loop(1, GROUPS, next_group, 0)

    def gather(side, block, window):
        where, which = inside[side, block], slot[side, block]
        results = None
        for k in range(blocks):
            parts = [take_lanes(source, where) for source in window(k)]
            here = which == k
            results = parts if k == 0 else [jnp.where(here, p, r) for p, r in zip(parts, results)]
        return results

    for way in range(2):
        send_jacobian(way).wait()
    for block in range(blocks):
        own = jac[4 + block]
        west = jnp.where(lane == 0, pltpu.roll(jac[3 + block], 1, 1), pltpu.roll(own, 1, 1))
        east = jnp.where(lane == LANES - 1, pltpu.roll(jac[5 + block], LANES - 1, 1), pltpu.roll(own, LANES - 1, 1))
        base = 8 * (block // 4)
        south, = gather(0, block, lambda k: [jac[base + k]])
        north, = gather(1, block, lambda k: [jac[base + k]])
        for s, other in enumerate((west, east, south, north)):
            scale[1 + s, block] = STEP_SIZE / (own + other)

    def second_part(group, carry):
        for way in range(2):
            send(way, group).wait()
        eastern = [[pltpu.roll(crossed[group, 0, 16], 1 + a, 1) for a in range(2)]]
        for block in range(blocks):
            cols = pl.ds(block * LANES, LANES)
            section, place = 1 + block // 4, (block % 4) * 4
            eastern.append([pltpu.roll(sides[group, 2 + a, block], 1, 1) for a in range(2)])
            if block == 0:
                western = [pltpu.roll(sides[group, a, 0], LANES - 1, 1) for a in range(2)]
            if block == blocks - 1:
                later = [pltpu.roll(crossed[group, 3, 16], LANES - 1 - a, 1) for a in range(2)]
            else:
                later = [pltpu.roll(sides[group, a, block + 1], LANES - 1, 1) for a in range(2)]
            others = [jnp.where(lane == 0, eastern[block][a], eastern[block + 1][a]) for a in range(2)]
            others += [jnp.where(lane == LANES - 1, later[a], western[a]) for a in range(2)]
            western = later
            for side in range(2):
                def window(k):
                    return [crossed[group, 2 * (block // 4) + k // 4, (k % 4) * 4 + 2 * side + c] for c in (1, 0)]
                others += gather(side, block, window)
            total = 0.0
            for k, n in enumerate(SIDES + CROSSED):
                own = sides[group, k, block] if k < 4 else crossed[group, section, place + k - 4]
                new = made[group, block, pl.ds(n, 8, stride=16), :] + scale[1 + k // 2, block] * (own + others[k])
                made[group, block, pl.ds(n, 8, stride=16), :] = new
                total = total + new
            q_ref[pl.ds(pl.multiple_of(group * 8, 8), 8), cols] += total * (5.0 / 144.0)
            held[group, :, cols] = made[group, block]
        deliver(group).start()
        return carry

    lax.fori_loop(0, GROUPS, second_part, 0)

    def finish(group, carry):
        deliver(group).wait()
        return carry

    lax.fori_loop(0, GROUPS, finish, 0)


def summands(x, count):
    parts = []
    for _ in range(count):
        parts.append(x.astype(jnp.bfloat16).astype(jnp.float32))
        x = x - parts[-1]
    return parts


def short_summands(x, count):
    parts = []
    for _ in range(count):
        big = x * float(2**20 + 1)
        parts.append(big - (big - x))
        x = x - parts[-1]
    return parts


def build_left(left, absorb, ray, solar):
    high, low = summands(absorb, 2)
    rays = short_summands(ray, 4)
    rays = rays + rays[:2]
    source = jnp.concatenate(
        [high, high, low] + rays + rays + summands(jnp.log2(solar), 3) + [jnp.zeros((G, 256 - LOGS - 3), jnp.float32)], axis=1
    ).astype(jnp.bfloat16)
    column = lax.broadcasted_iota(jnp.int32, (1, 256), 1)
    level_of = jnp.where(column < LEV, column, jnp.where(column < 2 * LEV, column - LEV, column - 2 * LEV))
    absorbs = column < EIGHTS
    eights = column < ONES
    ones = column < LOGS

    def one_step(step, carry):
        for i in range(STEP):
            level = LEV - 1 - step * STEP - i
            single = jnp.where(absorbs, jnp.where(level_of == level, 1.0, 0.0), jnp.where(eights, 0.0, jnp.where(ones, 1.0, 0.0)))
            tens = lax.div(level + 1, 8).astype(jnp.float32)
            units = lax.rem(level + 1, 8).astype(jnp.float32)
            rest = jnp.where(eights, tens, jnp.where(ones, units, 1.0))
            summed = jnp.where(absorbs, jnp.where(level_of <= level, 1.0, 0.0), rest)
            for kind, mask in enumerate((single, summed)):
                rows = pl.ds((kind * STEP + i) * G, G)
                left[step, rows, :] = source * jnp.broadcast_to(mask, (G, 256)).astype(jnp.bfloat16)
        return carry

    lax.fori_loop(0, STEPS, one_step, 0)


def build_right(square, ray_weights, log_weight):
    high, low = summands(square, 2)
    one = jnp.ones((1, LANES), jnp.float32)
    first, second_part = (one * part for part in ray_weights)
    weights = jnp.concatenate([first] * 4 + [second_part] * 2, axis=0)
    rows = [high, low, high, weights * 8.0, weights, jnp.broadcast_to(one * log_weight, (256 - LOGS, LANES))]
    return jnp.concatenate(rows, axis=0).astype(jnp.bfloat16)


def sublane_sums(arrays):
    row = lax.broadcasted_iota(jnp.int32, (8, LANES), 0)
    for size in (4, 2, 1):
        lower = (row & size) == 0
        joined = []
        for x, y in zip(arrays[:size], arrays[size:]):
            swapped = jnp.where(lower, y, x)
            if size == 4:
                moved = pltpu.roll(swapped, 4, 0)
            else:
                moved = jnp.where(lower, pltpu.roll(swapped, 8 - size, 0), pltpu.roll(swapped, size, 0))
            joined.append(jnp.where(lower, x, y) + moved)
        arrays = joined
    return arrays[0]


def radiate(
    q_hbm, mu_ref, alb_ref, lit_ref, absorb_ref, ray_ref, solar_ref, new_hbm, out_ref, kept_hbm,
    left, right, half_ray, top, even, odd, climbing, net, q_ref, new_ref, q_sem, new_sem, kept_sem,
):
    fetch = pltpu.make_async_copy(q_hbm, q_ref, q_sem)
    land = pltpu.make_async_copy(new_hbm, new_ref, new_sem)
    keep = pltpu.make_async_copy(new_ref, kept_hbm, kept_sem)
    fetch.start()
    land.start()
    lit_count = jnp.sum(lit_ref[...])
    pairs = E // (2 * LANES)

    @pl.when(lit_count > 0)
    def _():
        ray = ray_ref[...].T * EXPONENT
        solar = solar_ref[...].T
        build_left(left, absorb_ref[...].T * EXPONENT, ray, solar)
        half_ray[...] = jnp.broadcast_to(ray * 0.5, (G, LANES)).reshape(G_BLOCKS, 8, LANES)
        top[...] = jnp.broadcast_to(solar, (G, LANES)).reshape(G_BLOCKS, 8, LANES)

    fetch.wait()

    def columns(pair, b):
        return pl.ds(pl.multiple_of((2 * pair + b) * LANES, LANES), LANES)

    def depths(n, buffer, piece):
        pair, step = lax.div(n, STEPS), lax.rem(n, STEPS)
        size = 2 * STEP * G // 4
        rows = slice(piece * size, (piece + 1) * size)
        buffer[rows, :] = jnp.dot(left[step, rows, :], right[piece // 2, pair], preferred_element_type=jnp.float32)

    def climb(n, buffer, following, next_buffer):
        pair, step = lax.div(n, STEPS), lax.rem(n, STEPS)

        @pl.when(step == 0)
        def _():
            for b in range(2):
                climbing[b] = jnp.broadcast_to(alb_ref[0:1, columns(pair, b)][None], (G_BLOCKS, 8, LANES))

        below, totals = {}, {}
        for b in range(2):
            lanes = slice(b * LANES, (b + 1) * LANES)
            for half in range(2):
                below[half] = climbing[b, pl.ds(half * CHAINS, CHAINS)]
            for i in range(STEP):
                if i % (STEP // 2) == 0:
                    depths(following, next_buffer, 2 * b + i // (STEP // 2))
                level = LEV - 1 - step * STEP - i
                for half in range(2):
                    ray = half_ray[pl.ds(half * CHAINS, CHAINS)]
                    first = i * G + half * CHAINS * 8
                    second_kind = first + STEP * G
                    depth = buffer[first:first + CHAINS * 8, lanes].reshape(CHAINS, 8, LANES)
                    above_it = buffer[second_kind:second_kind + CHAINS * 8, lanes].reshape(CHAINS, 8, LANES)
                    totals[half] = jnp.sum(jnp.exp2(above_it) * (1.0 - below[half]), axis=0)
                    diffuse = jnp.exp2(depth)
                    reflect = (ray - ray * diffuse) * (1.0 / depth)
                    below[half] = reflect + diffuse * diffuse * below[half] * (1.0 / (1.0 - reflect * below[half]))
                net[b, level + 1] = totals[0] + totals[1]
            for half in range(2):
                climbing[b, pl.ds(half * CHAINS, CHAINS)] = below[half]

        @pl.when(step == STEPS - 1)
        def _():
            for b in range(2):
                cols = columns(pair, b)
                net[b, 0] = jnp.sum(top[...] * (1.0 - climbing[b]), axis=0)
                total = jnp.concatenate(
                    [sublane_sums([net[b, 8 * k + i] for i in range(8)]) for k in range(LEV // 8)]
                    + [jnp.sum(net[b, LEV], axis=0, keepdims=True)],
                    axis=0,
                )
                heat = (total[:LEV] - total[1:]) * (72.0 * mu_ref[0:1, cols])
                out_ref[:, cols] = jnp.where(lit_ref[0:1, cols] == 1, heat, 0.0)

    @pl.when(lit_count > 0)
    def _():
        for pair in range(pairs):
            for b in range(2):
                cols = slice((2 * pair + b) * LANES, (2 * pair + b + 1) * LANES)
                square = q_ref[:, cols]
                square = square * square
                slant = 1.0 / (1.66 * mu_ref[0:1, cols])
                lanes = slice(b * LANES, (b + 1) * LANES)
                right[0, pair, :, lanes] = build_right(square, (1.0, 0.0), 0.0)
                right[1, pair, :, lanes] = build_right(square * slant, summands(slant, 2), 1.0)
        for piece in range(4):
            depths(jnp.int32(0), even, piece)

        def two_steps(k, carry):
            @pl.when(k == 2)
            def _():
                land.wait()
                keep.start()

            climb(2 * k, even, 2 * k + 1, odd)
            climb(2 * k + 1, odd, jnp.minimum(2 * k + 2, pairs * STEPS - 1), even)
            return carry

        lax.fori_loop(0, pairs * STEPS // 2, two_steps, 0)

    @pl.when(lit_count == 0)
    def _():
        land.wait()
        keep.start()
        out_ref[...] = jnp.zeros((LEV, E), jnp.float32)

    keep.wait()


def shards(moisture, jacobian, partners, daylit, cos_zenith, albedo, absorb, rayleigh, solar):
    f32 = jnp.float32
    flat = moisture.reshape(LEV * 16, E)
    jac = jacobian.reshape(1, E)
    vmem, anywhere = pl.BlockSpec(memory_space=pltpu.VMEM), pl.BlockSpec(memory_space=pl.ANY)
    tile = (8, LANES)
    new, column_q = pl.pallas_call(
        exchange,
        in_specs=[anywhere] * 3,
        out_specs=[anywhere, vmem],
        out_shape=[jax.ShapeDtypeStruct((LEV * 16, E), f32), jax.ShapeDtypeStruct((LEV, E), f32)],
        scratch_shapes=[
            pltpu.VMEM((GROUPS, 128, E), f32),
            pltpu.VMEM((GROUPS, 8, 128, LANES), f32),
            pltpu.VMEM((GROUPS, 4, 8) + tile, f32),
            pltpu.VMEM((GROUPS, 4, 17) + tile, f32),
            pltpu.VMEM((16,) + tile, f32),
            pltpu.VMEM((5, 8) + tile, f32),
            pltpu.VMEM((2, 8) + tile, jnp.int32),
            pltpu.VMEM((2, 8) + tile, jnp.int32),
            pltpu.VMEM((1, E), f32),
            pltpu.VMEM((2, E), jnp.int32),
            pltpu.SemaphoreType.DMA((GROUPS + 2,)),
            pltpu.SemaphoreType.DMA((GROUPS,)),
            pltpu.SemaphoreType.DMA((2, GROUPS + 1)),
            pltpu.SemaphoreType.DMA((2, GROUPS + 1)),
        ],
        compiler_params=pltpu.CompilerParams(collective_id=0, has_side_effects=True, vmem_limit_bytes=60 * 2**20),
        name="exchange",
    )(flat, jac, partners)
    heating, new = pl.pallas_call(
        radiate,
        in_specs=[anywhere] + [vmem] * 6 + [anywhere],
        out_specs=[vmem, anywhere],
        out_shape=[jax.ShapeDtypeStruct((LEV, E), f32), jax.ShapeDtypeStruct((LEV * 16, E), f32)],
        scratch_shapes=[
            pltpu.VMEM((STEPS, 2 * STEP * G, 256), jnp.bfloat16),
            pltpu.VMEM((2, E // 256, 256, 256), jnp.bfloat16),
            pltpu.VMEM((G_BLOCKS,) + tile, f32),
            pltpu.VMEM((G_BLOCKS,) + tile, f32),
            pltpu.VMEM((2 * STEP * G, 256), f32),
            pltpu.VMEM((2 * STEP * G, 256), f32),
            pltpu.VMEM((2, G_BLOCKS) + tile, f32),
            pltpu.VMEM((2, LEV + 1) + tile, f32),
            pltpu.VMEM((LEV, E), f32),
            pltpu.VMEM((LEV * 16, E), f32),
            pltpu.SemaphoreType.DMA,
            pltpu.SemaphoreType.DMA,
            pltpu.SemaphoreType.DMA,
        ],
        compiler_params=pltpu.CompilerParams(vmem_limit_bytes=60 * 2**20),
        name="radiate",
    )(
        column_q,
        cos_zenith.reshape(1, E),
        albedo.reshape(1, E),
        daylit.reshape(1, E),
        absorb.T,
        rayleigh.reshape(1, G),
        solar.reshape(1, G),
        new,
    )
    return (new.reshape(LEV, 16, E), heating)


def solution(mesh):
    columns = P(("group", "curve"))
    placed = (
        P(None, None, ("group", "curve")),
        columns,
        P(None, ("group", "curve")),
        columns,
        columns,
        columns,
        P(),
        P(),
        P(),
    )
    return jax.shard_map(
        shards,
        mesh=mesh,
        in_specs=placed,
        out_specs=(P(None, None, ("group", "curve")), P(None, ("group", "curve"))),
        check_vma=False,
    )
```
